256 devices in a mesh: replica: 16 (over z_hi, y, core), fsdp: 16 (over z_lo, x).
Axes of the slice: x: 4, y: 4, z: 8 (z_hi: 2, z_lo: 4; z = z_hi * 4 + z_lo), core: 2. Of those that a mesh axis runs over, the one named last changes fastest.
Arguments:
- tokens: bfloat16 [131072, 4096], P(('replica', 'fsdp')), may hold values from -24 to 24
- key_grad: bfloat16 [131072, 1024], P(('replica', 'fsdp')), may hold values from -0.0625 to 0.0625
- key_weight: bfloat16 [16, 4096, 1024], P('replica', 'fsdp'), may hold values from -0.09375 to 0.09375
- adam_first: float32 [16, 4096, 1024], P('replica', 'fsdp'), may hold values from -4 to 4
- adam_second: float32 [16, 4096, 1024], P('replica', 'fsdp'), may hold values from 0.1 to 4
- local_params: bfloat16 [16, 4096, 1024], P('replica', 'fsdp'), may hold values from -4 to 4
- anchor: float32 [4096, 1024], P('fsdp'), may hold values from -4 to 4
- outer_momentum: float32 [4096, 1024], P('fsdp'), may hold values from -3 to 3
Outputs:
- keys: bfloat16 [131072, 1024], P(('replica', 'fsdp'))
- new_weight: bfloat16 [16, 4096, 1024], P('replica', 'fsdp')
- new_first: float32 [16, 4096, 1024], P('replica', 'fsdp')
- new_second: float32 [16, 4096, 1024], P('replica', 'fsdp')
- new_anchor: float32 [4096, 1024], P('fsdp')
- new_momentum: float32 [4096, 1024], P('fsdp')
The draws below stay inside these ranges and needn't reach their ends.
All inputs are finite; a program needn't handle non-finite values.
Results may differ from the reference program's by a relative error of at most 0.0085.
Values may be sent and summed in bfloat16 or wider, within the bound.
No kernel may reach another device: no remote copies, remote signals or barrier semaphores. Data moves between devices by JAX's collectives and lax.ppermute only.
A program may use at most 128 MiB of HBM per device.

```python
import math
import jax
import jax.numpy as jnp
from jax import lax

D = 4096
KV = 1024
TOK_DEV = 512
TOK_REP = 8192
TOKENS = 131072
N_REPLICA = 16
N_FSDP = 16


def strengthened(entries, own_key, source, target, shards_of, factor):
    owner, partner = [(jnp.arange(entries.shape[position]) // (entries.shape[position] // shards_of)).reshape([-1 if axis == position else 1 for axis in range(entries.ndim)]) for position in (source, target)]
    chosen = jax.random.permutation(own_key, shards_of)[partner]
    strong = (owner == chosen) | (owner == (partner + shards_of // 2) % shards_of)
    return jnp.where(strong, factor * entries, entries)


def shard_levels(rng, dims, split, least, largest):
    gain = 1.0
    for dim, parts in split:
        steps = jax.random.uniform(jax.random.fold_in(jax.random.fold_in(rng, 6), dim), (parts,), jnp.float32, least / len(split), largest / len(split))
        gain = gain * jnp.repeat(jnp.exp(steps), dims[dim] // parts).reshape((-1,) + (1,) * (len(dims) - 1 - dim))
    return gain


def bell_draw(own_key, shape, spread, most, cuts=(), kind=jnp.bfloat16):
    gain = shard_levels(own_key, shape, cuts, -0.22, 0.18) if cuts else 1.0
    array = jax.random.normal(own_key, shape, jnp.float32) * spread * gain
    return jnp.minimum(jnp.maximum(array, -most), most).astype(kind)


def gaussian_with(key, shape, scale, reach, cuts, heavy, dtype=jnp.bfloat16):
    values = scale * jax.random.normal(key, shape, jnp.float32)
    if cuts:
        values = values * shard_levels(key, shape, cuts, -0.22, 0.18)
    return jnp.clip(strengthened(values, jax.random.fold_in(key, 3), *heavy), -reach, reach).astype(dtype)


def setup_inputs(seed: int = 0) -> dict:
    seeds = jax.random.split(jax.random.key(seed), 9)
    return {
        "tokens": gaussian_with(seeds[0], (TOKENS, D), 1.0, 24.0, ((0, 256),), (0, 1, 256, 6.0)),
        "key_grad": bell_draw(seeds[1], (TOKENS, KV), (TOK_DEV * N_FSDP) ** -0.5, 0.0625, ((0, 256),)),
        "key_weight": bell_draw(seeds[2], (N_REPLICA, D, KV), D ** -0.5, 0.09375, ((0, 16), (1, 16))),
        "adam_first": bell_draw(seeds[3], (N_REPLICA, D, KV), 0.5, 4.0, ((0, 16), (1, 16)), jnp.float32),
        "adam_second": jnp.clip(jnp.exp(math.log(4.0) - 3.6888794 * jax.random.uniform(seeds[4], (N_REPLICA, D, KV), jnp.float32) ** shard_levels(seeds[4], (N_REPLICA, D, KV), ((0, 16), (1, 16)), -0.2, 0.2)), 0.1, 4.0),
        "local_params": bell_draw(seeds[5], (N_REPLICA, D, KV), 0.5, 4.0, ((0, 16), (1, 16))),
        "anchor": bell_draw(seeds[6], (D, KV), 0.5, 4.0, ((0, 16),), jnp.float32),
        "outer_momentum": bell_draw(seeds[7], (D, KV), 0.3, 3.0, ((0, 16),), jnp.float32),
    }


learn_rate = 0.001
weight_decay = 0.1
first_decay = 0.9
second_decay = 0.95
adam_floor = 1e-08
outer_rate = 0.7
outer_decay = 0.9

def inner_step(items):
    rows, cotangent, weight, first, second = items
    keys = jnp.dot(rows, weight, preferred_element_type=jnp.float32).astype(jnp.bfloat16)
    gradient = jnp.dot(rows.T, cotangent, preferred_element_type=jnp.float32)
    new_first = first_decay * first + (1.0 - first_decay) * gradient
    new_second = second_decay * second + (1.0 - second_decay) * gradient * gradient
    master = weight.astype(jnp.float32)
    update = new_first / (jnp.sqrt(new_second) + adam_floor) + weight_decay * master
    new_weight = (master - learn_rate * update).astype(jnp.bfloat16)
    return (keys, new_weight, new_first, new_second)

def reference(tokens, key_grad, key_weight, adam_first, adam_second, local_params, anchor, outer_momentum):
    rows = tokens.reshape(N_REPLICA, TOK_REP, D)
    cotangent = key_grad.reshape(N_REPLICA, TOK_REP, KV)
    keys, new_weight, new_first, new_second = lax.map(inner_step, (rows, cotangent, key_weight, adam_first, adam_second))
    drift = lax.optimization_barrier(jnp.sum(anchor[None] - local_params.astype(jnp.float32), axis=0)) / N_REPLICA
    new_momentum = outer_decay * outer_momentum + drift
    new_anchor = anchor - outer_rate * (drift + outer_decay * new_momentum)
    return (keys.reshape(TOKENS, KV), new_weight, new_first, new_second, new_anchor, new_momentum)
```

```python
import jax
import jax.numpy as jnp
from jax import lax
from jax.sharding import Mesh, PartitionSpec as P

learn_rate = 0.001
weight_decay = 0.1
first_decay = 0.9
second_decay = 0.95
adam_floor = 1e-08
outer_rate = 0.7
outer_decay = 0.9

bf16, f32 = jnp.bfloat16, jnp.float32
ALPHA = 128

HOME = (0, 1, 1, 0)
SWAP = [(c * 4 + x, (1 - c) * 4 + (x ^ 1)) for c in range(2) for x in range(4) if c != HOME[x]]
CORE = [(0, 1), (1, 0)]
ACROSS = [(x, 3 - x) for x in range(4)]
ENDS_IN = [(0, 1), (3, 2)]
ENDS_OUT = [(1, 0), (2, 3)]
PAIRS = ENDS_IN + ENDS_OUT
MIDDLE = [(1, 2), (2, 1)]
ORDER = ((3, 2, 1, 0), (3, 2, 0, 1), (0, 1, 3, 2), (0, 1, 2, 3))


def swap(v):
    return lax.ppermute(v, ("c", "x"), SWAP)


def core(v):
    return lax.ppermute(v, "c", CORE)


def across(v):
    return lax.ppermute(v, "x", ACROSS)


def line(v, pairs):
    return lax.ppermute(v, "zl", pairs)


def line_gather(own):
    beside = line(own, PAIRS)
    mid = line(own, MIDDLE)
    far = line(beside, MIDDLE)
    return [far + line(far, ENDS_OUT), mid + line(mid, ENDS_OUT), beside, own]


def dot(a, b):
    return jnp.dot(a, b, preferred_element_type=f32)


def dot_t(a, b):
    return lax.dot_general(a, b, (((0,), (0,)), ((), ())), preferred_element_type=f32)


def drift_sum(own, c, y, zh):
    def halve(v, axis, perm, bit, kind=f32):
        n = v.shape[0] // 2
        keep = lax.dynamic_slice_in_dim(v, bit * n, n, 0)
        send = lax.dynamic_slice_in_dim(v, (1 - bit) * n, n, 0).astype(kind)
        return keep + lax.ppermute(send, axis, perm).astype(f32)

    def double(v, axis, perm, bit):
        other = lax.ppermute(v, axis, perm)
        return jnp.where(bit == 0, jnp.concatenate([v, other]), jnp.concatenate([other, v]))

    near = [(i, i ^ 1) for i in range(4)]
    wide = [(i, i ^ 2) for i in range(4)]
    steps = (("c", CORE, c), ("y", near, y % 2), ("y", wide, y // 2))
    v = own
    for axis, perm, bit in steps:
        v = halve(v, axis, perm, bit)
    v = double(halve(v, "zh", CORE, zh, bf16), "zh", CORE, zh)
    for axis, perm, bit in steps[::-1]:
        v = double(v, axis, perm, bit)
    return v


def on_device(
    tokens, key_grad, key_weight, adam_first, adam_second, local_params, anchor, outer_momentum
):
    c, x, z, y, zh = (lax.axis_index(a) for a in ("c", "x", "zl", "y", "zh"))
    weight = key_weight[0]
    stays = c == jnp.where((x == 1) | (x == 2), 1, 0)
    mine = jnp.where(x < 2, c, 3 - c)
    theirs = jnp.where(x < 2, 1 - c, 2 + c)
    order = jnp.asarray(ORDER, jnp.int32)[z]

    def settle(v, arrived=None):
        return jnp.where(stays, v, swap(v) if arrived is None else arrived)

    w = settle(weight)
    g_own = settle(key_grad)
    blocks = [
        settle(lax.dynamic_slice_in_dim(tokens, order[k] * 1024, 1024, 1)) for k in range(4)
    ]
    g_other = core(g_own)

    def pick(v, quarter):
        return jnp.concatenate(
            [
                lax.dynamic_slice_in_dim(v, q * 256, 256, 1) for q in (quarter, 3 - quarter)
            ],
            axis=1,
        )

    x_own = [pick(b, mine) for b in blocks]
    x_other = [core(pick(b, theirs)) for b in blocks]

    first = line_gather(w[:ALPHA])
    low = [across(jnp.concatenate(first[2:])), across(jnp.concatenate(first[:2]))]
    low_far = [low[1][:ALPHA], low[1][ALPHA:], low[0][:ALPHA], low[0][ALPHA:]]
    rest = w[ALPHA:]
    second = line_gather(jnp.concatenate([rest, across(rest)]))
    n = 256 - ALPHA
    rows = [
        jnp.concatenate([first[k], second[k][:n], low_far[k], second[k][n:]]) for k in range(4)
    ]
    halves = [sum(dot(xs[k], rows[k]) for k in (3, 2, 1, 0)) for xs in (x_own, x_other)]
    keys_work = (halves[0] + core(halves[1].astype(bf16)).astype(f32)).astype(bf16)
    keys = settle(keys_work)

    part = []
    for k in range(4):
        whole = dot_t(x_own[k], g_own) + dot_t(x_other[k], g_other)
        part.append(whole[:256] + across(whole[256:].astype(bf16)).astype(f32))
    send = lambda v, pairs: line(v.astype(bf16), pairs).astype(f32)
    r0 = send(part[0], ENDS_IN)
    r1 = send(part[1], ENDS_IN)
    r2 = send(part[2], ENDS_IN)
    m0 = send(part[0] + r0, MIDDLE)
    m1 = send(part[1] + r1, MIDDLE)
    e0 = send(part[2] + m0, ENDS_OUT)
    total = part[3] + r2 + m1 + e0
    gradient = jnp.where(stays, total, swap(total.astype(bf16)).astype(f32))

    new_first = first_decay * adam_first[0] + (1.0 - first_decay) * gradient
    new_second = second_decay * adam_second[0] + (1.0 - second_decay) * gradient * gradient
    master = weight.astype(f32)
    update = new_first / (jnp.sqrt(new_second) + adam_floor) + weight_decay * master
    new_weight = (master - learn_rate * update).astype(bf16)

    drift = drift_sum(anchor - local_params[0].astype(f32), c, y, zh) / 16
    new_momentum = outer_decay * outer_momentum + drift
    new_anchor = anchor - outer_rate * (drift + outer_decay * new_momentum)
    return (keys, new_weight[None], new_first[None], new_second[None], new_anchor, new_momentum)


def solution(mesh):
    fine = Mesh(mesh.devices.reshape(2, 4, 2, 4, 4), ("zh", "y", "c", "zl", "x"))
    replica, fsdp = ("zh", "y", "c"), ("zl", "x")
    tokens, stacked, shared = P(replica + fsdp, None), P(replica, fsdp, None), P(fsdp, None)
    return jax.shard_map(
        on_device,
        mesh=fine,
        in_specs=(tokens, tokens, stacked, stacked, stacked, stacked, shared, shared),
        out_specs=(tokens, stacked, stacked, stacked, shared, shared),
        check_vma=False,
    )
```

```python
import jax
import jax.numpy as jnp
from jax import lax
from jax.sharding import Mesh, PartitionSpec as P

learn_rate = 0.001
weight_decay = 0.1
first_decay = 0.9
second_decay = 0.95
adam_floor = 1e-08
outer_rate = 0.7
outer_decay = 0.9

bf16, f32 = jnp.bfloat16, jnp.float32
ALPHA = 96

HOME = (0, 1, 1, 0)
SWAP = [(c * 4 + x, (1 - c) * 4 + (x ^ 1)) for c in range(2) for x in range(4) if c != HOME[x]]
CORE = [(0, 1), (1, 0)]
ACROSS = [(x, 3 - x) for x in range(4)]
BESIDE = [(x, x ^ 1) for x in range(4)]
ENDS_OUT = [(1, 0), (2, 3)]
PAIRS = [(0, 1), (1, 0), (2, 3), (3, 2)]
MIDDLE = [(1, 2), (2, 1)]
ORDER = ((3, 2, 1, 0), (3, 2, 0, 1), (0, 1, 3, 2), (0, 1, 2, 3))


def swap(v):
    return lax.ppermute(v, ("c", "x"), SWAP)


def core(v):
    return lax.ppermute(v, "c", CORE)


def beside(v):
    return lax.ppermute(v, "x", BESIDE)


def across(v):
    return lax.ppermute(v, "x", ACROSS)


def line(v, pairs):
    return lax.ppermute(v, "zl", pairs)


def dot(a, b):
    return jnp.dot(a, b, preferred_element_type=f32)


def dot_t(a, b):
    return lax.dot_general(a, b, (((0,), (0,)), ((), ())), preferred_element_type=f32)


def together(*arrays):
    return lax.optimization_barrier(arrays)


class Drift:
    def __init__(self, own, c, y, zh):
        near = [(i, i ^ 1) for i in range(4)]
        wide = [(i, i ^ 2) for i in range(4)]
        self.v = own
        self.steps = [("c", CORE, c), ("y", near, y % 2), ("y", wide, y // 2), ("zh", CORE, zh)]
        self.at = 0

    def send(self):
        if self.at < 4:
            bit = self.steps[self.at][2]
            n = self.v.shape[0] // 2
            sent = lax.dynamic_slice_in_dim(self.v, (1 - bit) * n, n, 0)
            return sent.astype(bf16) if self.at == 3 else sent
        return self.v

    def step(self, sent):
        axis, perm, _ = self.steps[min(self.at, 7 - self.at)]
        return lax.ppermute(sent, axis, perm)

    def take(self, got):
        bit = self.steps[min(self.at, 7 - self.at)][2]
        if self.at < 4:
            n = self.v.shape[0] // 2
            self.v = lax.dynamic_slice_in_dim(self.v, bit * n, n, 0) + got.astype(f32)
        else:
            v = self.v
            self.v = jnp.where(bit == 0, jnp.concatenate([v, got]), jnp.concatenate([got, v]))
        self.at += 1


def on_device(
    tokens, key_grad, key_weight, adam_first, adam_second, local_params, anchor, outer_momentum
):
    c, x, z, y, zh = (lax.axis_index(a) for a in ("c", "x", "zl", "y", "zh"))
    weight = key_weight[0]
    stays = c == jnp.where((x == 1) | (x == 2), 1, 0)
    end = (z == 0) | (z == 3)
    mine = jnp.where(x < 2, c, 3 - c)
    theirs = jnp.where(x < 2, 1 - c, 2 + c)
    order = [
        jnp.where(z < 2, 3, 0),
        jnp.where(z < 2, 2, 1),
        jnp.where(z == 0, 1, jnp.where(z == 1, 0, jnp.where(z == 2, 3, 2))),
        z,
    ]

    def half(quarter):
        return jnp.concatenate(
            [
                lax.dynamic_slice_in_dim(tokens, order[k] * 1024 + q * 256, 256, 1)
                for k in range(4)
                for q in (quarter, 3 - quarter)
            ],
            axis=1,
        )

    w = jnp.where(stays, weight, swap(weight))
    g_sib = core(key_grad)
    x_own, x_sib = half(mine), core(half(theirs))
    drift = Drift(anchor - local_params[0].astype(f32), c, y, zh)
    drift.take(drift.step(drift.send()))
    x_a = jnp.where(stays, x_own, x_sib)
    x_l = jnp.where(stays, x_sib, x_own)
    g_a = jnp.where(stays, key_grad, g_sib)
    g_l = lax.dynamic_slice_in_dim(jnp.where(stays, g_sib, key_grad), c * 256, 256, 0)
    leave = [x_l[:, 512 * k : 512 * k + 512] for k in range(4)]
    keep = [x_a[:, 512 * k : 512 * k + 512] for k in range(4)]
    base = [dot_t(k, g_a) for k in keep]

    got = (beside(g_l), across(w), line(w, PAIRS), line(w, MIDDLE), drift.step(drift.send()))
    got, leave, drift.v = together(got, leave, drift.v)
    g_half, q_own, e_own, m_own, d = got
    drift.take(d)

    g_rest = core(g_half)
    g_b = jnp.where(
        c == 0, jnp.concatenate([g_half, g_rest]), jnp.concatenate([g_rest, g_half])
    )
    q_beta = q_own[ALPHA:]
    pad = jnp.zeros((ALPHA, 1024), bf16)
    got = (
        beside(leave[0]),
        line(jnp.where(end, jnp.concatenate([q_beta, pad]), m_own), PAIRS),
        line(e_own, MIDDLE),
        across(e_own[:ALPHA]),
        drift.step(drift.send()),
    )
    got, leave, drift.v, g_b = together(got, leave, drift.v, g_b)
    x_b = [got[0]]
    _, e2, m2, q2, d = got
    drift.take(d)

    def whole(k):
        v = base[k] + dot_t(x_b[k], g_b)
        return v[:256], v[256:].astype(bf16)

    mid = jnp.where(end, e2, m_own)
    stay0, go0 = whole(0)
    got = (
        beside(leave[1]),
        line(m2, ENDS_OUT),
        line(q_beta, MIDDLE),
        across(jnp.concatenate([go0, mid[:ALPHA]])),
        drift.step(drift.send()),
    )
    got, leave, drift.v, stay0 = together(got, leave, drift.v, stay0)
    x_b.append(got[0])
    _, e3, m3, q3, d = got
    drift.take(d)
    part0 = stay0 + q3[:256].astype(f32)

    far = jnp.where(end, e3, m2)
    stay1, go1 = whole(1)
    cut = 256 - (256 - ALPHA)
    got = (
        beside(leave[2]),
        line(
            jnp.where(end, part0.astype(bf16), jnp.concatenate([q_beta, m3[:cut]])), PAIRS
        ),
        line(e2[: 256 - ALPHA], MIDDLE),
        across(jnp.concatenate([go1, far[:ALPHA]])),
        drift.step(drift.send()),
    )
    got, leave, drift.v, stay1, part0 = together(got, leave, drift.v, stay1, part0)
    x_b.append(got[0])
    _, e4, m4, q4, d = got
    drift.take(d)
    part1 = stay1 + q4[:256].astype(f32)

    stay2, go2 = whole(2)
    fill = jnp.zeros((2 * ALPHA + cut - 256, 1024), bf16)
    got = (
        beside(leave[3]),
        line(
            jnp.where(
                end, part1.astype(bf16), jnp.concatenate([m3[cut:], m4, fill])
            ),
            PAIRS,
        ),
        line((part0 + e4.astype(f32)).astype(bf16), MIDDLE),
        across(go2),
        drift.step(drift.send()),
    )
    got, drift.v, stay2, part1 = together(got, drift.v, stay2, part1)
    x_b.append(got[0])
    _, e5, m5, q5, d = got
    drift.take(d)
    part2 = stay2 + q5.astype(f32)

    n = 256 - ALPHA
    beta1 = jnp.where(end, jnp.concatenate([e4[n:], e5[: n - cut]]), m3)
    beta0 = jnp.where(end, e5[n - cut : 2 * n - cut], m4)
    beta2 = jnp.where(end, e4[:n], e2[:n])
    rows = [
        jnp.concatenate([far, q4[256:], beta0]),
        jnp.concatenate([mid, q3[256:], beta1]),
        jnp.concatenate([e_own, q2, beta2]),
        jnp.concatenate([w, q_own]),
    ]
    k_a = sum(dot(keep[k], rows[k]) for k in (3, 2, 1, 0))
    k_b = sum(dot(x_b[k], rows[k]) for k in (2, 1, 0, 3))
    k_got = core(jnp.where(stays, k_b, k_a).astype(bf16))
    keys_work = (jnp.where(stays, k_a, k_b) + k_got.astype(f32)).astype(bf16)

    stay3, go3 = whole(3)
    got = (
        swap(keys_work),
        line((part2 + m5.astype(f32)).astype(bf16), PAIRS),
        line((part1 + e5.astype(f32)).astype(bf16), MIDDLE),
        across(go3),
        drift.step(drift.send()),
    )
    k_back, e6, m6, q6, d = got
    drift.take(d)
    keys = jnp.where(stays, keys_work, k_back)
    total = stay3 + q6.astype(f32) + e6.astype(f32) + m6.astype(f32)
    gradient = jnp.where(stays, total, swap(total.astype(bf16)).astype(f32))
    drift.take(drift.step(drift.send()))

    new_first = first_decay * adam_first[0] + (1.0 - first_decay) * gradient
    new_second = second_decay * adam_second[0] + (1.0 - second_decay) * gradient * gradient
    master = weight.astype(f32)
    update = new_first / (jnp.sqrt(new_second) + adam_floor) + weight_decay * master
    new_weight = (master - learn_rate * update).astype(bf16)

    mean = drift.v / 16
    new_momentum = outer_decay * outer_momentum + mean
    new_anchor = anchor - outer_rate * (mean + outer_decay * new_momentum)
    return (keys, new_weight[None], new_first[None], new_second[None], new_anchor, new_momentum)


def solution(mesh):
    fine = Mesh(mesh.devices.reshape(2, 4, 2, 4, 4), ("zh", "y", "c", "zl", "x"))
    replica, fsdp = ("zh", "y", "c"), ("zl", "x")
    tokens, stacked, shared = P(replica + fsdp, None), P(replica, fsdp, None), P(fsdp, None)
    return jax.shard_map(
        on_device,
        mesh=fine,
        in_specs=(tokens, tokens, stacked, stacked, stacked, stacked, shared, shared),
        out_specs=(tokens, stacked, stacked, stacked, shared, shared),
        check_vma=False,
    )
```

```python
import jax
import jax.numpy as jnp
from jax import lax
from jax.experimental import pallas as pl
from jax.experimental.pallas import tpu as pltpu
from jax.sharding import Mesh, PartitionSpec as P

learn_rate = 0.001
weight_decay = 0.1
first_decay = 0.9
second_decay = 0.95
adam_floor = 1e-08
outer_rate = 0.7
outer_decay = 0.9

bf16, f32 = jnp.bfloat16, jnp.float32

HOME = (0, 1, 1, 0)
SWAP = [(c * 4 + x, (1 - c) * 4 + (x ^ 1)) for c in range(2) for x in range(4) if c != HOME[x]]
CORE = [(0, 1), (1, 0)]
ACROSS = [(x, 3 - x) for x in range(4)]
BESIDE = [(x, x ^ 1) for x in range(4)]
ENDS_OUT = [(1, 0), (2, 3)]
PAIRS = [(0, 1), (1, 0), (2, 3), (3, 2)]
MIDDLE = [(1, 2), (2, 1)]
ORDER = ((3, 2, 1, 0), (3, 2, 0, 1), (0, 1, 3, 2), (0, 1, 2, 3))


def swap(v):
    return lax.ppermute(v, ("c", "x"), SWAP)


def core(v):
    return lax.ppermute(v, "c", CORE)


def beside(v):
    return lax.ppermute(v, "x", BESIDE)


def across(v):
    return lax.ppermute(v, "x", ACROSS)


def line(v, pairs):
    return lax.ppermute(v, "zl", pairs)


def dot(a, b):
    return jnp.dot(a, b, preferred_element_type=f32)


def dot_t(a, b):
    return lax.dot_general(a, b, (((0,), (0,)), ((), ())), preferred_element_type=f32)


def together(*arrays):
    return lax.optimization_barrier(arrays)


def move(_, a, b, to_a, to_b):
    to_a[0] = a[...]
    to_b[0] = b[...]


def halves(tokens, blocks):
    spec = lambda i: pl.BlockSpec((512, 256), lambda n, table: (0, table[i, n]))
    out = pl.BlockSpec((1, 512, 256), lambda n, table: (n // 2, 0, n % 2))
    kind = jax.ShapeDtypeStruct((4, 512, 512), bf16)
    return pl.pallas_call(
        move,
        grid_spec=pltpu.PrefetchScalarGridSpec(
            num_scalar_prefetch=1,
            grid=(8,),
            in_specs=[spec(0), spec(1)],
            out_specs=[out, out],
        ),
        out_shape=[kind, kind],
        cost_estimate=pl.CostEstimate(flops=0, bytes_accessed=16 << 20, transcendentals=0),
    )(blocks, tokens, tokens)


class Drift:
    def __init__(self, own, c, y):
        near = [(i, i ^ 1) for i in range(4)]
        wide = [(i, i ^ 2) for i in range(4)]
        self.v = own
        self.steps = [("c", CORE, c), ("y", near, y % 2), ("y", wide, y // 2), ("zh", CORE, c)]
        self.at = 0

    def send(self):
        if self.at < 3:
            bit = self.steps[self.at][2]
            n = self.v.shape[0] // 2
            self.sent = lax.dynamic_slice_in_dim(self.v, (1 - bit) * n, n, 0)
        elif self.at == 3:
            (self.sent,) = together(self.v.astype(bf16))
        else:
            self.sent = self.v
        axis, perm, _ = self.steps[min(self.at, 6 - self.at)]
        return lax.ppermute(self.sent, axis, perm)

    def take(self, got):
        bit = self.steps[min(self.at, 6 - self.at)][2]
        v = self.v
        if self.at < 3:
            n = v.shape[0] // 2
            self.v = lax.dynamic_slice_in_dim(v, bit * n, n, 0) + got
        elif self.at == 3:
            self.v = self.sent.astype(f32) + got.astype(f32)
        else:
            self.v = jnp.where(bit == 0, jnp.concatenate([v, got]), jnp.concatenate([got, v]))
        self.at += 1


def on_device(
    tokens, key_grad, key_weight, adam_first, adam_second, local_params, anchor, outer_momentum
):
    c, x, z, y = (lax.axis_index(a) for a in ("c", "x", "zl", "y"))
    weight = key_weight[0]
    stays = c == jnp.where((x == 1) | (x == 2), 1, 0)
    end = (z == 0) | (z == 3)
    mine = jnp.where(x < 2, c, 3 - c)
    theirs = jnp.where(x < 2, 1 - c, 2 + c)
    order = [
        jnp.where(z < 2, 3, 0),
        jnp.where(z < 2, 2, 1),
        jnp.where(z == 0, 1, jnp.where(z == 1, 0, jnp.where(z == 2, 3, 2))),
        z,
    ]
    blocks = jnp.stack(
        [4 * order[k] + q for half in (theirs, mine) for k in range(4) for q in (half, 3 - half)]
    ).reshape(2, 8)

    w = jnp.where(stays, weight, swap(weight))
    g_sib = core(key_grad)
    x_give, x_own = halves(tokens, blocks.astype(jnp.int32))
    x_sib = core(x_give)
    drift = Drift(anchor - local_params[0].astype(f32), c, y)
    drift.take(drift.send())
    g_a = jnp.where(stays, key_grad, g_sib)
    g_l = lax.dynamic_slice_in_dim(jnp.where(stays, g_sib, key_grad), c * 256, 256, 0)

    got = (beside(g_l), line(w, PAIRS), line(w, MIDDLE), across(w), drift.send())
    leave = [jnp.where(stays, x_sib[k], x_own[k]) for k in range(4)]
    keep = [jnp.where(stays, x_own[k], x_sib[k]) for k in range(4)]
    got, leave, drift.v = together(got, leave, drift.v)
    g_half, e_own, m_own, q_own, d = got
    drift.take(d)

    got = (beside(leave[0]), line(m_own, ENDS_OUT), line(e_own, MIDDLE), across(e_own), drift.send())
    g_rest = core(g_half)
    g_b = jnp.where(
        c == 0, jnp.concatenate([g_half, g_rest]), jnp.concatenate([g_rest, g_half])
    )
    base = [dot_t(k, g_a) for k in keep]
    sent = drift.v
    got, leave, sent, g_b, base = together(got, leave, sent, g_b, base)
    drift.v = sent
    x_b = [got[0]]
    _, e2, m2, q2, d = got
    drift.take(d)
    mid = jnp.where(end, e2, m_own)

    def going(k):
        return (base[k][256:] + dot_t(x_b[k][:, 256:], g_b)).astype(bf16)

    def staying(k):
        return base[k][:256] + dot_t(x_b[k][:, :256], g_b)

    def cat(*arrays):
        return jnp.concatenate(arrays, axis=-1)

    got = (beside(leave[1]), line(m2, ENDS_OUT), line(q_own, MIDDLE), across(going(0)), drift.send())
    rows = [None, None, jnp.concatenate([e_own, q2]), jnp.concatenate([w, q_own])]
    k_a = dot(cat(keep[2], keep[3]), jnp.concatenate(rows[2:]))
    stay = staying(0)
    got, leave, drift.v, drift.sent, stay, k_a = together(got, leave, drift.v, drift.sent, stay, k_a)
    x_b.append(got[0])
    _, e3, m3, q3, d = got
    drift.take(d)
    part0 = stay + q3.astype(f32)

    got = (
        beside(leave[2]),
        line(jnp.where(end, part0.astype(bf16), m3), PAIRS),
        line(q2, MIDDLE),
        across(going(1)),
        drift.send(),
    )
    stay = staying(1)
    got, leave, drift.v, stay, part0 = together(got, leave, drift.v, stay, part0)
    x_b.append(got[0])
    _, e4, m4, q4, d = got
    drift.take(d)
    part1 = stay + q4.astype(f32)

    got = (
        beside(leave[3]),
        line(jnp.where(end, part1.astype(bf16), m4), PAIRS),
        line((part0 + e4.astype(f32)).astype(bf16), MIDDLE),
        across(going(2)),
        drift.send(),
    )
    rows[1] = jnp.concatenate([mid, jnp.where(end, e4, m3)])
    k_a = k_a + dot(keep[1], rows[1])
    k_b = dot(cat(x_b[1], x_b[2]), jnp.concatenate(rows[1:3]))
    stay = staying(2)
    got, drift.v, stay, part1, k_a, k_b = together(got, drift.v, stay, part1, k_a, k_b)
    x_b.append(got[0])
    _, e5, m5, q5, d = got
    drift.take(d)
    part2 = stay + q5.astype(f32)

    got = (
        line((part2 + m5.astype(f32)).astype(bf16), PAIRS),
        line((part1 + e5.astype(f32)).astype(bf16), MIDDLE),
        across(going(3)),
    )
    rows[0] = jnp.concatenate([jnp.where(end, e3, m2), jnp.where(end, e5, m4)])
    k_a = k_a + dot(keep[0], rows[0])
    k_b = k_b + dot(cat(x_b[0], x_b[3]), jnp.concatenate([rows[0], rows[3]]))
    k_got = core(jnp.where(stays, k_b, k_a).astype(bf16))
    keys_work = (jnp.where(stays, k_a, k_b) + k_got.astype(f32)).astype(bf16)
    keys = jnp.where(stays, keys_work, swap(keys_work))
    e6, m6, q6 = got
    total = staying(3) + q6.astype(f32) + e6.astype(f32) + m6.astype(f32)
    gradient = jnp.where(stays, total, swap(total.astype(bf16)).astype(f32))
    drift.take(drift.send())

    new_first = first_decay * adam_first[0] + (1.0 - first_decay) * gradient
    new_second = second_decay * adam_second[0] + (1.0 - second_decay) * gradient * gradient
    master = weight.astype(f32)
    update = new_first / (jnp.sqrt(new_second) + adam_floor) + weight_decay * master
    new_weight = (master - learn_rate * update).astype(bf16)

    mean = drift.v / 16
    new_momentum = outer_decay * outer_momentum + mean
    new_anchor = anchor - outer_rate * (mean + outer_decay * new_momentum)
    return (keys, new_weight[None], new_first[None], new_second[None], new_anchor, new_momentum)


def solution(mesh):
    fine = Mesh(mesh.devices.reshape(2, 4, 2, 4, 4), ("zh", "y", "c", "zl", "x"))
    replica, fsdp = ("zh", "y", "c"), ("zl", "x")
    tokens, stacked, shared = P(replica + fsdp, None), P(replica, fsdp, None), P(fsdp, None)
    return jax.shard_map(
        on_device,
        mesh=fine,
        in_specs=(tokens, tokens, stacked, stacked, stacked, stacked, shared, shared),
        out_specs=(tokens, stacked, stacked, stacked, shared, shared),
        check_vma=False,
    )
```

```python
import jax
import jax.numpy as jnp
from jax import lax
from jax.experimental import pallas as pl
from jax.experimental.pallas import tpu as pltpu
from jax.sharding import Mesh, PartitionSpec as P

learn_rate = 0.001
weight_decay = 0.1
first_decay = 0.9
second_decay = 0.95
adam_floor = 1e-08
outer_rate = 0.7
outer_decay = 0.9

bf16, f32 = jnp.bfloat16, jnp.float32

HOME = (0, 1, 1, 0)
SWAP = [(c * 4 + x, (1 - c) * 4 + (x ^ 1)) for c in range(2) for x in range(4) if c != HOME[x]]
CORE = [(0, 1), (1, 0)]
ACROSS = [(x, 3 - x) for x in range(4)]
BESIDE = [(x, x ^ 1) for x in range(4)]
ENDS_OUT = [(1, 0), (2, 3)]
PAIRS = [(0, 1), (1, 0), (2, 3), (3, 2)]
MIDDLE = [(1, 2), (2, 1)]
ORDER = ((3, 2, 1, 0), (3, 2, 0, 1), (0, 1, 3, 2), (0, 1, 2, 3))


def swap(v):
    return lax.ppermute(v, ("c", "x"), SWAP)


def core(v):
    return lax.ppermute(v, "c", CORE)


def beside(v):
    return lax.ppermute(v, "x", BESIDE)


def across(v):
    return lax.ppermute(v, "x", ACROSS)


def line(v, pairs):
    return lax.ppermute(v, "zl", pairs)


def dot(a, b):
    return jnp.dot(a, b, preferred_element_type=f32)


def dot_t(a, b):
    return lax.dot_general(a, b, (((0,), (0,)), ((), ())), preferred_element_type=f32)


def together(*arrays):
    return lax.optimization_barrier(arrays)


def sort_columns(table, own, sib, leave, keep):
    stays = table[8] == 1
    leave[0] = jnp.where(stays, sib[...], own[...])
    keep[0] = jnp.where(stays, own[...], sib[...])


def halves(table, own, sib):
    block = pl.BlockSpec((512, 256), lambda n, table: (0, table[n]))
    out = pl.BlockSpec((1, 512, 256), lambda n, table: (n // 2, 0, n % 2))
    kind = jax.ShapeDtypeStruct((4, 512, 512), bf16)
    return pl.pallas_call(
        sort_columns,
        grid_spec=pltpu.PrefetchScalarGridSpec(
            num_scalar_prefetch=1, grid=(8,), in_specs=[block, block], out_specs=[out, out]
        ),
        out_shape=[kind, kind],
        cost_estimate=pl.CostEstimate(flops=0, bytes_accessed=0, transcendentals=0),
    )(table, own, sib)


class Drift:
    def __init__(self, own, c, y):
        near = [(i, i ^ 1) for i in range(4)]
        wide = [(i, i ^ 2) for i in range(4)]
        self.v = own
        self.steps = [("c", CORE, c), ("y", near, y % 2), ("y", wide, y // 2), ("zh", CORE, c)]
        self.at = 0

    def send(self, after):
        self.v, _ = together(self.v, after)
        if self.at < 3:
            bit = self.steps[self.at][2]
            n = self.v.shape[0] // 2
            self.sent = lax.dynamic_slice_in_dim(self.v, (1 - bit) * n, n, 0)
        elif self.at == 3:
            (self.sent,) = together(self.v.astype(bf16))
        else:
            self.sent = self.v
        axis, perm, _ = self.steps[min(self.at, 6 - self.at)]
        return lax.ppermute(self.sent, axis, perm)

    def take(self, got):
        bit = self.steps[min(self.at, 6 - self.at)][2]
        v = self.v
        if self.at < 3:
            n = v.shape[0] // 2
            self.v = lax.dynamic_slice_in_dim(v, bit * n, n, 0) + got
        elif self.at == 3:
            self.v = self.sent.astype(f32) + got.astype(f32)
        else:
            self.v = jnp.where(bit == 0, jnp.concatenate([v, got]), jnp.concatenate([got, v]))
        self.at += 1


def on_device(
    tokens, key_grad, key_weight, adam_first, adam_second, local_params, anchor, outer_momentum
):
    c, x, z, y = (lax.axis_index(a) for a in ("c", "x", "zl", "y"))
    weight = key_weight[0]
    stays = c == jnp.where((x == 1) | (x == 2), 1, 0)
    end = (z == 0) | (z == 3)
    mine = jnp.where(x < 2, c, 3 - c)
    order = [
        jnp.where(z < 2, 3, 0),
        jnp.where(z < 2, 2, 1),
        jnp.where(z == 0, 1, jnp.where(z == 1, 0, jnp.where(z == 2, 3, 2))),
        z,
    ]
    table = jnp.stack(
        [4 * order[k] + q for k in range(4) for q in (mine, 3 - mine)] + [stays.astype(jnp.int32)]
    ).astype(jnp.int32)

    w = jnp.where(stays, weight, swap(weight))
    g_mine = lax.dynamic_slice_in_dim(key_grad, c * 256, 256, 0)
    g_first = core(lax.dynamic_slice_in_dim(key_grad, (1 - c) * 256, 256, 0))
    g_l = jnp.where(stays, g_first, g_mine)
    x_sib = core(tokens)
    drift = Drift(anchor - local_params[0].astype(f32), c, y)
    drift.take(drift.send(w))

    x_l, x_k = halves(table, tokens, x_sib)
    leave, keep = ([v[k] for k in range(4)] for v in (x_l, x_k))
    g_mine, _ = together(g_mine, x_sib)
    g_second = core(g_mine)
    got = (beside(g_l), line(w, PAIRS), line(w, MIDDLE), across(w), drift.send(leave[0]))
    got, leave, g_second, drift.v = together(got, leave, g_second, drift.v)
    g_half, e_own, m_own, q_own, d = got
    drift.take(d)

    def in_order(a, b):
        return jnp.where(c == 0, jnp.concatenate([a, b]), jnp.concatenate([b, a]))

    g_a = jnp.where(stays, key_grad, in_order(g_first, g_second))
    g_b = in_order(g_half, core(g_half))
    g_a, g_b = together(g_a, g_b)
    base = [dot_t(k, g_a) for k in keep]
    got = (
        beside(leave[0]),
        line(m_own, ENDS_OUT),
        line(e_own, MIDDLE),
        across(e_own),
        drift.send(g_b),
    )
    sent = drift.v
    got, leave, sent, g_b, base = together(got, leave, sent, g_b, base)
    drift.v = sent
    x_b = [got[0]]
    _, e2, m2, q2, d = got
    drift.take(d)
    mid = jnp.where(end, e2, m_own)

    def going(k):
        return (base[k][256:] + dot_t(x_b[k][:, 256:], g_b)).astype(bf16)

    def staying(k):
        return base[k][:256] + dot_t(x_b[k][:, :256], g_b)

    def cat(*arrays):
        return jnp.concatenate(arrays, axis=-1)

    stay = staying(0)
    got = (
        beside(leave[1]),
        line(m2, ENDS_OUT),
        line(q_own, MIDDLE),
        across(going(0)),
        drift.send(stay),
    )
    rows = [None, None, jnp.concatenate([e_own, q2]), jnp.concatenate([w, q_own])]
    k_a = dot(cat(keep[2], keep[3]), jnp.concatenate(rows[2:]))
    got, leave, drift.v, drift.sent, stay, k_a = together(got, leave, drift.v, drift.sent, stay, k_a)
    x_b.append(got[0])
    _, e3, m3, q3, d = got
    drift.take(d)
    part0 = stay + q3.astype(f32)

    stay = staying(1)
    got = (
        beside(leave[2]),
        line(jnp.where(end, part0.astype(bf16), m3), PAIRS),
        line(q2, MIDDLE),
        across(going(1)),
        drift.send(stay),
    )
    got, leave, drift.v, stay, part0 = together(got, leave, drift.v, stay, part0)
    x_b.append(got[0])
    _, e4, m4, q4, d = got
    drift.take(d)
    part1 = stay + q4.astype(f32)

    stay = staying(2)
    rows[1] = jnp.concatenate([mid, jnp.where(end, e4, m3)])
    k_a = k_a + dot(keep[1], rows[1])
    k_b = dot(cat(x_b[1], x_b[2]), jnp.concatenate(rows[1:3]))
    got = (
        beside(leave[3]),
        line(jnp.where(end, part1.astype(bf16), m4), PAIRS),
        line((part0 + e4.astype(f32)).astype(bf16), MIDDLE),
        across(going(2)),
    )
    got, stay, part1, k_a, k_b = together(got, stay, part1, k_a, k_b)
    x_b.append(got[0])
    _, e5, m5, q5 = got
    part2 = stay + q5.astype(f32)

    got = (
        line((part2 + m5.astype(f32)).astype(bf16), PAIRS),
        line((part1 + e5.astype(f32)).astype(bf16), MIDDLE),
        across(going(3)),
    )
    rows[0] = jnp.concatenate([jnp.where(end, e3, m2), jnp.where(end, e5, m4)])
    k_a = k_a + dot(keep[0], rows[0])
    k_b = k_b + dot(cat(x_b[0], x_b[3]), jnp.concatenate([rows[0], rows[3]]))
    k_got = core(jnp.where(stays, k_b, k_a).astype(bf16))
    keys_work = (jnp.where(stays, k_a, k_b) + k_got.astype(f32)).astype(bf16)
    k_back = swap(keys_work)
    drift.take(drift.send(keys_work))
    keys = jnp.where(stays, keys_work, k_back)
    (e6, m6, q6), _ = together(got, k_back)
    total = staying(3) + q6.astype(f32) + e6.astype(f32) + m6.astype(f32)
    gradient = jnp.where(stays, total, swap(total.astype(bf16)).astype(f32))
    drift.take(drift.send(k_back))

    new_first = first_decay * adam_first[0] + (1.0 - first_decay) * gradient
    new_second = second_decay * adam_second[0] + (1.0 - second_decay) * gradient * gradient
    master = weight.astype(f32)
    update = new_first / (jnp.sqrt(new_second) + adam_floor) + weight_decay * master
    new_weight = (master - learn_rate * update).astype(bf16)

    mean = drift.v / 16
    new_momentum = outer_decay * outer_momentum + mean
    new_anchor = anchor - outer_rate * (mean + outer_decay * new_momentum)
    return (keys, new_weight[None], new_first[None], new_second[None], new_anchor, new_momentum)


def solution(mesh):
    fine = Mesh(mesh.devices.reshape(2, 4, 2, 4, 4), ("zh", "y", "c", "zl", "x"))
    replica, fsdp = ("zh", "y", "c"), ("zl", "x")
    tokens, stacked, shared = P(replica + fsdp, None), P(replica, fsdp, None), P(fsdp, None)
    return jax.shard_map(
        on_device,
        mesh=fine,
        in_specs=(tokens, tokens, stacked, stacked, stacked, stacked, shared, shared),
        out_specs=(tokens, stacked, stacked, stacked, shared, shared),
        check_vma=False,
    )
```

```python
import jax
import jax.numpy as jnp
from jax import lax
from jax.experimental import pallas as pl
from jax.experimental.pallas import tpu as pltpu
from jax.sharding import Mesh, PartitionSpec as P

learn_rate = 0.001
weight_decay = 0.1
first_decay = 0.9
second_decay = 0.95
adam_floor = 1e-08
outer_rate = 0.7
outer_decay = 0.9

bf16, f32 = jnp.bfloat16, jnp.float32

HOME = (0, 1, 1, 0)
SWAP = [(c * 4 + x, (1 - c) * 4 + (x ^ 1)) for c in range(2) for x in range(4) if c != HOME[x]]
CORE = [(0, 1), (1, 0)]
ACROSS = [(x, 3 - x) for x in range(4)]
BESIDE = [(x, x ^ 1) for x in range(4)]
ENDS_OUT = [(1, 0), (2, 3)]
PAIRS = [(0, 1), (1, 0), (2, 3), (3, 2)]
MIDDLE = [(1, 2), (2, 1)]
ORDER = ((3, 2, 1, 0), (3, 2, 0, 1), (0, 1, 3, 2), (0, 1, 2, 3))


def swap(v):
    return lax.ppermute(v, ("c", "x"), SWAP)


def core(v):
    return lax.ppermute(v, "c", CORE)


def beside(v):
    return lax.ppermute(v, "x", BESIDE)


def across(v):
    return lax.ppermute(v, "x", ACROSS)


def line(v, pairs):
    return lax.ppermute(v, "zl", pairs)


def dot(a, b):
    return jnp.dot(a, b, preferred_element_type=f32)


def dot_t(a, b):
    return lax.dot_general(a, b, (((0,), (0,)), ((), ())), preferred_element_type=f32)


def together(*arrays):
    return lax.optimization_barrier(arrays)


def sort_columns(table, tokens, give, own, sems):
    copies = []
    for half, out in enumerate((give, own)):
        for n in range(8):
            column = pl.multiple_of(table[half, n] * 256, 256)
            copies.append(
                pltpu.make_async_copy(
                    tokens.at[:, pl.ds(column, 256)],
                    out.at[n // 2, :, pl.ds(n % 2 * 256, 256)],
                    sems.at[half, n],
                )
            )
    for copy in copies:
        copy.start()
    for copy in copies:
        copy.wait()


def halves(tokens, table):
    kind = jax.ShapeDtypeStruct((4, 512, 512), bf16)
    anywhere = pl.BlockSpec(memory_space=pl.ANY)
    return pl.pallas_call(
        sort_columns,
        grid_spec=pltpu.PrefetchScalarGridSpec(
            num_scalar_prefetch=1,
            grid=(1,),
            in_specs=[anywhere],
            out_specs=[anywhere, anywhere],
            scratch_shapes=[pltpu.SemaphoreType.DMA((2, 8))],
        ),
        out_shape=[kind, kind],
        cost_estimate=pl.CostEstimate(flops=0, bytes_accessed=8 << 20, transcendentals=0),
    )(table, tokens)


class Drift:
    def __init__(self, own, c, y):
        near = [(i, i ^ 1) for i in range(4)]
        wide = [(i, i ^ 2) for i in range(4)]
        self.v = own
        self.steps = [("c", CORE, c), ("y", near, y % 2), ("y", wide, y // 2), ("zh", CORE, c)]
        self.at = 0

    def send(self):
        if self.at < 3:
            bit = self.steps[self.at][2]
            n = self.v.shape[0] // 2
            self.sent = lax.dynamic_slice_in_dim(self.v, (1 - bit) * n, n, 0)
        elif self.at == 3:
            (self.sent,) = together(self.v.astype(bf16))
        else:
            self.sent = self.v
        axis, perm, _ = self.steps[min(self.at, 6 - self.at)]
        return lax.ppermute(self.sent, axis, perm)

    def take(self, got):
        bit = self.steps[min(self.at, 6 - self.at)][2]
        v = self.v
        if self.at < 3:
            n = v.shape[0] // 2
            self.v = lax.dynamic_slice_in_dim(v, bit * n, n, 0) + got
        elif self.at == 3:
            self.v = self.sent.astype(f32) + got.astype(f32)
        else:
            self.v = jnp.where(bit == 0, jnp.concatenate([v, got]), jnp.concatenate([got, v]))
        self.at += 1


def on_device(
    tokens, key_grad, key_weight, adam_first, adam_second, local_params, anchor, outer_momentum
):
    c, x, z, y = (lax.axis_index(a) for a in ("c", "x", "zl", "y"))
    weight = key_weight[0]
    stays = c == jnp.where((x == 1) | (x == 2), 1, 0)
    end = (z == 0) | (z == 3)
    mine = jnp.where(x < 2, c, 3 - c)
    theirs = jnp.where(x < 2, 1 - c, 2 + c)
    order = [
        jnp.where(z < 2, 3, 0),
        jnp.where(z < 2, 2, 1),
        jnp.where(z == 0, 1, jnp.where(z == 1, 0, jnp.where(z == 2, 3, 2))),
        z,
    ]
    blocks = jnp.stack(
        [4 * order[k] + q for half in (theirs, mine) for k in range(4) for q in (half, 3 - half)]
    ).reshape(2, 8)

    w = jnp.where(stays, weight, swap(weight))
    g_mine = lax.dynamic_slice_in_dim(key_grad, c * 256, 256, 0)
    g_first = core(lax.dynamic_slice_in_dim(key_grad, (1 - c) * 256, 256, 0))
    g_l = jnp.where(stays, g_first, g_mine)
    drift = Drift(anchor - local_params[0].astype(f32), c, y)
    d = drift.send()
    blocks = blocks.astype(jnp.int32)
    w, g_l, g_mine, g_first, blocks, d, drift.v = together(
        w, g_l, g_mine, g_first, blocks, d, drift.v
    )
    drift.take(d)

    x_give, x_own = halves(tokens, blocks)
    x_sib = core(x_give)
    got = (beside(g_l), line(w, PAIRS), line(w, MIDDLE), across(w), drift.send())
    leave = [jnp.where(stays, x_sib[k], x_own[k]) for k in range(4)]
    keep = [jnp.where(stays, x_own[k], x_sib[k]) for k in range(4)]
    got, leave, g_mine, drift.v = together(got, leave, g_mine, drift.v)
    g_half, e_own, m_own, q_own, d = got
    drift.take(d)

    got = (beside(leave[0]), line(m_own, ENDS_OUT), line(e_own, MIDDLE), across(e_own), drift.send())
    rest = core(jnp.concatenate([g_half, g_mine]))

    def in_order(a, b):
        return jnp.where(c == 0, jnp.concatenate([a, b]), jnp.concatenate([b, a]))

    g_b = in_order(g_half, rest[:256])
    g_a = jnp.where(stays, key_grad, in_order(g_first, rest[256:]))
    base = [dot_t(k, g_a) for k in keep]
    sent = drift.v
    got, leave, sent, g_b, base = together(got, leave, sent, g_b, base)
    drift.v = sent
    x_b = [got[0]]
    _, e2, m2, q2, d = got
    drift.take(d)
    mid = jnp.where(end, e2, m_own)

    def going(k):
        return (base[k][256:] + dot_t(x_b[k][:, 256:], g_b)).astype(bf16)

    def staying(k):
        return base[k][:256] + dot_t(x_b[k][:, :256], g_b)

    def cat(*arrays):
        return jnp.concatenate(arrays, axis=-1)

    got = (beside(leave[1]), line(m2, ENDS_OUT), line(q_own, MIDDLE), across(going(0)), drift.send())
    rows = [None, None, jnp.concatenate([e_own, q2]), jnp.concatenate([w, q_own])]
    k_a = dot(cat(keep[2], keep[3]), jnp.concatenate(rows[2:]))
    stay = staying(0)
    got, leave, drift.v, drift.sent, stay, k_a = together(got, leave, drift.v, drift.sent, stay, k_a)
    x_b.append(got[0])
    _, e3, m3, q3, d = got
    drift.take(d)
    part0 = stay + q3.astype(f32)

    got = (
        beside(leave[2]),
        line(jnp.where(end, part0.astype(bf16), m3), PAIRS),
        line(q2, MIDDLE),
        across(going(1)),
        drift.send(),
    )
    stay = staying(1)
    got, leave, drift.v, stay, part0 = together(got, leave, drift.v, stay, part0)
    x_b.append(got[0])
    _, e4, m4, q4, d = got
    drift.take(d)
    part1 = stay + q4.astype(f32)

    got = (
        beside(leave[3]),
        line(jnp.where(end, part1.astype(bf16), m4), PAIRS),
        line((part0 + e4.astype(f32)).astype(bf16), MIDDLE),
        across(going(2)),
        drift.send(),
    )
    rows[1] = jnp.concatenate([mid, jnp.where(end, e4, m3)])
    k_a = k_a + dot(keep[1], rows[1])
    k_b = dot(cat(x_b[1], x_b[2]), jnp.concatenate(rows[1:3]))
    stay = staying(2)
    got, drift.v, stay, part1, k_a, k_b = together(got, drift.v, stay, part1, k_a, k_b)
    x_b.append(got[0])
    _, e5, m5, q5, d = got
    drift.take(d)
    part2 = stay + q5.astype(f32)

    got = (
        line((part2 + m5.astype(f32)).astype(bf16), PAIRS),
        line((part1 + e5.astype(f32)).astype(bf16), MIDDLE),
        across(going(3)),
    )
    rows[0] = jnp.concatenate([jnp.where(end, e3, m2), jnp.where(end, e5, m4)])
    k_a = k_a + dot(keep[0], rows[0])
    k_b = k_b + dot(cat(x_b[0], x_b[3]), jnp.concatenate([rows[0], rows[3]]))
    k_got = core(jnp.where(stays, k_b, k_a).astype(bf16))
    keys_work = (jnp.where(stays, k_a, k_b) + k_got.astype(f32)).astype(bf16)
    keys = jnp.where(stays, keys_work, swap(keys_work))
    e6, m6, q6 = got
    total = staying(3) + q6.astype(f32) + e6.astype(f32) + m6.astype(f32)
    gradient = jnp.where(stays, total, swap(total.astype(bf16)).astype(f32))
    drift.take(drift.send())

    new_first = first_decay * adam_first[0] + (1.0 - first_decay) * gradient
    new_second = second_decay * adam_second[0] + (1.0 - second_decay) * gradient * gradient
    master = weight.astype(f32)
    update = new_first / (jnp.sqrt(new_second) + adam_floor) + weight_decay * master
    new_weight = (master - learn_rate * update).astype(bf16)

    mean = drift.v / 16
    new_momentum = outer_decay * outer_momentum + mean
    new_anchor = anchor - outer_rate * (mean + outer_decay * new_momentum)
    return (keys, new_weight[None], new_first[None], new_second[None], new_anchor, new_momentum)


def solution(mesh):
    fine = Mesh(mesh.devices.reshape(2, 4, 2, 4, 4), ("zh", "y", "c", "zl", "x"))
    replica, fsdp = ("zh", "y", "c"), ("zl", "x")
    tokens, stacked, shared = P(replica + fsdp, None), P(replica, fsdp, None), P(fsdp, None)
    return jax.shard_map(
        on_device,
        mesh=fine,
        in_specs=(tokens, tokens, stacked, stacked, stacked, stacked, shared, shared),
        out_specs=(tokens, stacked, stacked, stacked, shared, shared),
        check_vma=False,
    )
```

```python
import jax
import jax.numpy as jnp
from jax import lax
from jax.experimental import pallas as pl
from jax.experimental.pallas import tpu as pltpu
from jax.sharding import Mesh, PartitionSpec as P

learn_rate = 0.001
weight_decay = 0.1
first_decay = 0.9
second_decay = 0.95
adam_floor = 1e-08
outer_rate = 0.7
outer_decay = 0.9

bf16, f32 = jnp.bfloat16, jnp.float32

HOME = (0, 1, 1, 0)
SWAP = [(c * 4 + x, (1 - c) * 4 + (x ^ 1)) for c in range(2) for x in range(4) if c != HOME[x]]
CORE = [(0, 1), (1, 0)]
ACROSS = [(x, 3 - x) for x in range(4)]
BESIDE = [(x, x ^ 1) for x in range(4)]
ENDS_OUT = [(1, 0), (2, 3)]
PAIRS = [(0, 1), (1, 0), (2, 3), (3, 2)]
MIDDLE = [(1, 2), (2, 1)]
ORDER = ((3, 2, 1, 0), (3, 2, 0, 1), (0, 1, 3, 2), (0, 1, 2, 3))


def swap(v):
    return lax.ppermute(v, ("c", "x"), SWAP)


def core(v):
    return lax.ppermute(v, "c", CORE)


def beside(v):
    return lax.ppermute(v, "x", BESIDE)


def across(v):
    return lax.ppermute(v, "x", ACROSS)


def line(v, pairs):
    return lax.ppermute(v, "zl", pairs)


def dot(a, b):
    return jnp.dot(a, b, preferred_element_type=f32)


def dot_t(a, b):
    return lax.dot_general(a, b, (((0,), (0,)), ((), ())), preferred_element_type=f32)


def together(*arrays):
    return lax.optimization_barrier(arrays)


def after(array, *earlier):
    return together(array, *earlier)[0]


def move(_, a, b, to_a, to_b):
    to_a[0] = a[...]
    to_b[0] = b[...]


def halves(tokens, blocks):
    spec = lambda i: pl.BlockSpec((512, 256), lambda n, table: (0, table[i, n]))
    out = pl.BlockSpec((1, 512, 256), lambda n, table: (n // 2, 0, n % 2))
    kind = jax.ShapeDtypeStruct((4, 512, 512), bf16)
    return pl.pallas_call(
        move,
        grid_spec=pltpu.PrefetchScalarGridSpec(
            num_scalar_prefetch=1,
            grid=(8,),
            in_specs=[spec(0), spec(1)],
            out_specs=[out, out],
        ),
        out_shape=[kind, kind],
        cost_estimate=pl.CostEstimate(flops=0, bytes_accessed=0, transcendentals=0),
    )(blocks, tokens, tokens)


class Drift:
    def __init__(self, own, c, y):
        near = [(i, i ^ 1) for i in range(4)]
        wide = [(i, i ^ 2) for i in range(4)]
        self.v = own
        self.steps = [("c", CORE, c), ("y", near, y % 2), ("y", wide, y // 2), ("zh", CORE, c)]
        self.at = 0

    def send(self, earlier):
        self.v = after(self.v, earlier)
        if self.at < 3:
            bit = self.steps[self.at][2]
            n = self.v.shape[0] // 2
            self.sent = lax.dynamic_slice_in_dim(self.v, (1 - bit) * n, n, 0)
        elif self.at == 3:
            (self.sent,) = together(self.v.astype(bf16))
        else:
            self.sent = self.v
        axis, perm, _ = self.steps[min(self.at, 6 - self.at)]
        return lax.ppermute(self.sent, axis, perm)

    def take(self, got):
        bit = self.steps[min(self.at, 6 - self.at)][2]
        v = self.v
        if self.at < 3:
            n = v.shape[0] // 2
            self.v = lax.dynamic_slice_in_dim(v, bit * n, n, 0) + got
        elif self.at == 3:
            self.v = self.sent.astype(f32) + got.astype(f32)
        else:
            self.v = jnp.where(bit == 0, jnp.concatenate([v, got]), jnp.concatenate([got, v]))
        self.at += 1


def on_device(
    tokens, key_grad, key_weight, adam_first, adam_second, local_params, anchor, outer_momentum
):
    c, x, z, y = (lax.axis_index(a) for a in ("c", "x", "zl", "y"))
    weight = key_weight[0]
    stays = c == jnp.where((x == 1) | (x == 2), 1, 0)
    end = (z == 0) | (z == 3)
    mine = jnp.where(x < 2, c, 3 - c)
    theirs = jnp.where(x < 2, 1 - c, 2 + c)
    order = [
        jnp.where(z < 2, 3, 0),
        jnp.where(z < 2, 2, 1),
        jnp.where(z == 0, 1, jnp.where(z == 1, 0, jnp.where(z == 2, 3, 2))),
        z,
    ]
    blocks = jnp.stack(
        [4 * order[k] + q for half in (theirs, mine) for k in range(4) for q in (half, 3 - half)]
    ).reshape(2, 8)

    w = jnp.where(stays, weight, swap(weight))
    g_mine = lax.dynamic_slice_in_dim(key_grad, c * 256, 256, 0)
    g_first = core(lax.dynamic_slice_in_dim(key_grad, (1 - c) * 256, 256, 0))
    g_l = jnp.where(stays, g_first, g_mine)
    drift = Drift(anchor - local_params[0].astype(f32), c, y)
    d = drift.send(g_l)
    w, g_l, blocks, d = together(w, g_l, blocks.astype(jnp.int32), d)
    drift.take(d)

    g_half, e_own, m_own, q_own = beside(g_l), line(w, PAIRS), line(w, MIDDLE), across(w)
    x_give, x_own = halves(tokens, blocks)
    x_sib = core(x_give)
    drift.take(drift.send(w))
    leave = [jnp.where(stays, x_sib[k], x_own[k]) for k in range(4)]
    keep = [jnp.where(stays, x_own[k], x_sib[k]) for k in range(4)]

    x_b = [beside(after(leave[0], g_half))]
    e2 = line(after(m_own, e_own, g_half, leave[0]), ENDS_OUT)
    m2 = line(after(e_own, m_own, g_half, leave[0]), MIDDLE)
    q2 = across(after(e_own, q_own, g_half, leave[0]))
    drift.take(drift.send(g_half))
    rest = core(jnp.concatenate([g_half, g_mine]))

    def in_order(a, b):
        return jnp.where(c == 0, jnp.concatenate([a, b]), jnp.concatenate([b, a]))

    g_b = in_order(g_half, rest[:256])
    g_a = jnp.where(stays, key_grad, in_order(g_first, rest[256:]))
    base = [dot_t(k, g_a) for k in keep]
    mid = jnp.where(end, e2, m_own)

    def going(k):
        return (base[k][256:] + dot_t(x_b[k][:, 256:], g_b)).astype(bf16)

    def staying(k):
        return base[k][:256] + dot_t(x_b[k][:, :256], g_b)

    def cat(*arrays):
        return jnp.concatenate(arrays, axis=-1)

    x_b.append(beside(after(leave[1], x_b[0])))
    e3 = line(after(m2, e2, x_b[0]), ENDS_OUT)
    m3 = line(after(q_own, m2, x_b[0]), MIDDLE)
    q3 = across(after(going(0), q2))
    drift.take(drift.send(x_b[0]))
    rows = [None, None, jnp.concatenate([e_own, q2]), jnp.concatenate([w, q_own])]
    k_a = dot(cat(keep[2], keep[3]), jnp.concatenate(rows[2:]))
    part0 = staying(0) + q3.astype(f32)

    x_b.append(beside(after(leave[2], x_b[1])))
    e4 = line(after(jnp.where(end, part0.astype(bf16), m3), e3, x_b[1]), PAIRS)
    m4 = line(after(q2, m3, x_b[1]), MIDDLE)
    q4 = across(after(going(1), q3))
    drift.take(drift.send(x_b[1]))
    part1 = staying(1) + q4.astype(f32)

    x_b.append(beside(after(leave[3], x_b[2])))
    e5 = line(after(jnp.where(end, part1.astype(bf16), m4), e4, x_b[2]), PAIRS)
    m5 = line(after((part0 + e4.astype(f32)).astype(bf16), m4, x_b[2]), MIDDLE)
    q5 = across(after(going(2), q4))
    drift.take(drift.send(x_b[2]))
    rows[1] = jnp.concatenate([mid, jnp.where(end, e4, m3)])
    k_a = k_a + dot(keep[1], rows[1])
    k_b = dot(cat(x_b[1], x_b[2]), jnp.concatenate(rows[1:3]))
    part2 = staying(2) + q5.astype(f32)

    e6 = line(after((part2 + m5.astype(f32)).astype(bf16), e5), PAIRS)
    m6 = line(after((part1 + e5.astype(f32)).astype(bf16), m5), MIDDLE)
    q6 = across(after(going(3), q5))
    rows[0] = jnp.concatenate([jnp.where(end, e3, m2), jnp.where(end, e5, m4)])
    k_a = k_a + dot(keep[0], rows[0])
    k_b = k_b + dot(cat(x_b[0], x_b[3]), jnp.concatenate([rows[0], rows[3]]))
    k_got = core(jnp.where(stays, k_b, k_a).astype(bf16))
    keys_work = (jnp.where(stays, k_a, k_b) + k_got.astype(f32)).astype(bf16)
    keys = jnp.where(stays, keys_work, swap(keys_work))
    total = staying(3) + q6.astype(f32) + e6.astype(f32) + m6.astype(f32)
    gradient = jnp.where(stays, total, swap(total.astype(bf16)).astype(f32))
    drift.take(drift.send(x_b[3]))

    new_first = first_decay * adam_first[0] + (1.0 - first_decay) * gradient
    new_second = second_decay * adam_second[0] + (1.0 - second_decay) * gradient * gradient
    master = weight.astype(f32)
    update = new_first / (jnp.sqrt(new_second) + adam_floor) + weight_decay * master
    new_weight = (master - learn_rate * update).astype(bf16)

    mean = drift.v / 16
    new_momentum = outer_decay * outer_momentum + mean
    new_anchor = anchor - outer_rate * (mean + outer_decay * new_momentum)
    return (keys, new_weight[None], new_first[None], new_second[None], new_anchor, new_momentum)


def solution(mesh):
    fine = Mesh(mesh.devices.reshape(2, 4, 2, 4, 4), ("zh", "y", "c", "zl", "x"))
    replica, fsdp = ("zh", "y", "c"), ("zl", "x")
    tokens, stacked, shared = P(replica + fsdp, None), P(replica, fsdp, None), P(fsdp, None)
    return jax.shard_map(
        on_device,
        mesh=fine,
        in_specs=(tokens, tokens, stacked, stacked, stacked, stacked, shared, shared),
        out_specs=(tokens, stacked, stacked, stacked, shared, shared),
        check_vma=False,
    )
```

```python
import jax
import jax.numpy as jnp
from jax import lax
from jax.experimental import pallas as pl
from jax.experimental.pallas import tpu as pltpu
from jax.sharding import Mesh, PartitionSpec as P

learn_rate = 0.001
weight_decay = 0.1
first_decay = 0.9
second_decay = 0.95
adam_floor = 1e-08
outer_rate = 0.7
outer_decay = 0.9

bf16, f32 = jnp.bfloat16, jnp.float32

HOME = (0, 1, 1, 0)
SWAP = [(c * 4 + x, (1 - c) * 4 + (x ^ 1)) for c in range(2) for x in range(4) if c != HOME[x]]
CORE = [(0, 1), (1, 0)]
ACROSS = [(x, 3 - x) for x in range(4)]
BESIDE = [(x, x ^ 1) for x in range(4)]
ENDS_OUT = [(1, 0), (2, 3)]
PAIRS = [(0, 1), (1, 0), (2, 3), (3, 2)]
MIDDLE = [(1, 2), (2, 1)]
ORDER = ((3, 2, 1, 0), (3, 2, 0, 1), (0, 1, 3, 2), (0, 1, 2, 3))


def swap(v):
    return lax.ppermute(v, ("c", "x"), SWAP)


def core(v):
    return lax.ppermute(v, "c", CORE)


def beside(v):
    return lax.ppermute(v, "x", BESIDE)


def across(v):
    return lax.ppermute(v, "x", ACROSS)


def line(v, pairs):
    return lax.ppermute(v, "zl", pairs)


def dot(a, b):
    return jnp.dot(a, b, preferred_element_type=f32)


def dot_t(a, b):
    return lax.dot_general(a, b, (((0,), (0,)), ((), ())), preferred_element_type=f32)


def together(*arrays):
    return lax.optimization_barrier(arrays)


def after(array, *earlier):
    return together(array, *earlier)[0]


def move(_, a, b, to_a, to_b):
    to_a[0] = a[...]
    to_b[0] = b[...]


def halves(tokens, blocks):
    spec = lambda i: pl.BlockSpec((512, 256), lambda n, table: (0, table[i, n]))
    out = pl.BlockSpec((1, 512, 256), lambda n, table: (n // 2, 0, n % 2))
    kind = jax.ShapeDtypeStruct((4, 512, 512), bf16)
    return pl.pallas_call(
        move,
        grid_spec=pltpu.PrefetchScalarGridSpec(
            num_scalar_prefetch=1,
            grid=(8,),
            in_specs=[spec(0), spec(1)],
            out_specs=[out, out],
        ),
        out_shape=[kind, kind],
        cost_estimate=pl.CostEstimate(flops=0, bytes_accessed=16 << 20, transcendentals=0),
    )(blocks, tokens, tokens)


class Drift:
    def __init__(self, own, c, y):
        near = [(i, i ^ 1) for i in range(4)]
        wide = [(i, i ^ 2) for i in range(4)]
        self.v = own
        self.steps = [("c", CORE, c), ("y", near, y % 2), ("y", wide, y // 2), ("zh", CORE, c)]
        self.at = 0

    def send(self, *earlier):
        self.v = after(self.v, *earlier)
        if self.at < 3:
            bit = self.steps[self.at][2]
            n = self.v.shape[0] // 2
            self.sent = lax.dynamic_slice_in_dim(self.v, (1 - bit) * n, n, 0)
        elif self.at == 3:
            (self.sent,) = together(self.v.astype(bf16))
        else:
            self.sent = self.v
        axis, perm, _ = self.steps[min(self.at, 6 - self.at)]
        return lax.ppermute(self.sent, axis, perm)

    def take(self, got):
        bit = self.steps[min(self.at, 6 - self.at)][2]
        v = self.v
        if self.at < 3:
            n = v.shape[0] // 2
            self.v = lax.dynamic_slice_in_dim(v, bit * n, n, 0) + got
        elif self.at == 3:
            self.v = self.sent.astype(f32) + got.astype(f32)
        else:
            self.v = jnp.where(bit == 0, jnp.concatenate([v, got]), jnp.concatenate([got, v]))
        self.at += 1


def on_device(
    tokens, key_grad, key_weight, adam_first, adam_second, local_params, anchor, outer_momentum
):
    c, x, z, y = (lax.axis_index(a) for a in ("c", "x", "zl", "y"))
    weight = key_weight[0]
    stays = c == jnp.where((x == 1) | (x == 2), 1, 0)
    end = (z == 0) | (z == 3)
    mine = jnp.where(x < 2, c, 3 - c)
    theirs = jnp.where(x < 2, 1 - c, 2 + c)
    order = [
        jnp.where(z < 2, 3, 0),
        jnp.where(z < 2, 2, 1),
        jnp.where(z == 0, 1, jnp.where(z == 1, 0, jnp.where(z == 2, 3, 2))),
        z,
    ]
    blocks = jnp.stack(
        [4 * order[k] + q for half in (theirs, mine) for k in range(4) for q in (half, 3 - half)]
    ).reshape(2, 8)

    w = jnp.where(stays, weight, swap(weight))
    g_sib = core(key_grad)
    x_give, x_own = halves(tokens, blocks.astype(jnp.int32))
    x_sib = core(x_give)
    drift = Drift(anchor - local_params[0].astype(f32), c, y)
    drift.take(drift.send())
    w, g_sib = together(w, g_sib)
    g_a = jnp.where(stays, key_grad, g_sib)
    g_l = lax.dynamic_slice_in_dim(jnp.where(stays, g_sib, key_grad), c * 256, 256, 0)

    got = (beside(g_l), line(w, PAIRS), line(w, MIDDLE), across(w), drift.send())
    leave = [jnp.where(stays, x_sib[k], x_own[k]) for k in range(4)]
    keep = [jnp.where(stays, x_own[k], x_sib[k]) for k in range(4)]
    got, leave, drift.v = together(got, leave, drift.v)
    g_half, e_own, m_own, q_own, d = got
    drift.take(d)

    x_b = [beside(leave[0])]
    e2, m2, q2 = line(m_own, ENDS_OUT), line(e_own, MIDDLE), across(e_own)
    drift.take(drift.send(g_half))
    g_rest = core(g_half)
    g_b = jnp.where(
        c == 0, jnp.concatenate([g_half, g_rest]), jnp.concatenate([g_rest, g_half])
    )
    base = [dot_t(k, g_a) for k in keep]
    mid = jnp.where(end, e2, m_own)

    def going(k):
        return (base[k][256:] + dot_t(x_b[k][:, 256:], g_b)).astype(bf16)

    def staying(k):
        return base[k][:256] + dot_t(x_b[k][:, :256], g_b)

    def cat(*arrays):
        return jnp.concatenate(arrays, axis=-1)

    x_b.append(beside(after(leave[1], x_b[0])))
    e3 = line(after(m2, e2, x_b[0]), ENDS_OUT)
    m3 = line(after(q_own, m2, x_b[0]), MIDDLE)
    q3 = across(after(going(0), q2))
    drift.take(drift.send(x_b[0]))
    rows = [None, None, jnp.concatenate([e_own, q2]), jnp.concatenate([w, q_own])]
    k_a = dot(cat(keep[2], keep[3]), jnp.concatenate(rows[2:]))
    part0 = staying(0) + q3.astype(f32)

    x_b.append(beside(after(leave[2], x_b[1])))
    e4 = line(after(jnp.where(end, part0.astype(bf16), m3), e3, x_b[1]), PAIRS)
    m4 = line(after(q2, m3, x_b[1]), MIDDLE)
    q4 = across(after(going(1), q3))
    drift.take(drift.send(x_b[1]))
    part1 = staying(1) + q4.astype(f32)

    x_b.append(beside(after(leave[3], x_b[2])))
    e5 = line(after(jnp.where(end, part1.astype(bf16), m4), e4, x_b[2]), PAIRS)
    m5 = line(after((part0 + e4.astype(f32)).astype(bf16), m4, x_b[2]), MIDDLE)
    q5 = across(after(going(2), q4))
    drift.take(drift.send(x_b[2]))
    rows[1] = jnp.concatenate([mid, jnp.where(end, e4, m3)])
    k_a = k_a + dot(keep[1], rows[1])
    k_b = dot(cat(x_b[1], x_b[2]), jnp.concatenate(rows[1:3]))
    part2 = staying(2) + q5.astype(f32)
    (x_b[3], e5, m5, q5), drift.v, part1, part2, k_a, k_b = together(
        (x_b[3], e5, m5, q5), drift.v, part1, part2, k_a, k_b
    )

    got = (
        line((part2 + m5.astype(f32)).astype(bf16), PAIRS),
        line((part1 + e5.astype(f32)).astype(bf16), MIDDLE),
        across(going(3)),
    )
    rows[0] = jnp.concatenate([jnp.where(end, e3, m2), jnp.where(end, e5, m4)])
    k_a = k_a + dot(keep[0], rows[0])
    k_b = k_b + dot(cat(x_b[0], x_b[3]), jnp.concatenate([rows[0], rows[3]]))
    k_got = core(jnp.where(stays, k_b, k_a).astype(bf16))
    keys_work = (jnp.where(stays, k_a, k_b) + k_got.astype(f32)).astype(bf16)
    keys = jnp.where(stays, keys_work, swap(keys_work))
    e6, m6, q6 = got
    total = staying(3) + q6.astype(f32) + e6.astype(f32) + m6.astype(f32)
    gradient = jnp.where(stays, total, swap(total.astype(bf16)).astype(f32))
    drift.take(drift.send())

    new_first = first_decay * adam_first[0] + (1.0 - first_decay) * gradient
    new_second = second_decay * adam_second[0] + (1.0 - second_decay) * gradient * gradient
    master = weight.astype(f32)
    update = new_first / (jnp.sqrt(new_second) + adam_floor) + weight_decay * master
    new_weight = (master - learn_rate * update).astype(bf16)

    mean = drift.v / 16
    new_momentum = outer_decay * outer_momentum + mean
    new_anchor = anchor - outer_rate * (mean + outer_decay * new_momentum)
    return (keys, new_weight[None], new_first[None], new_second[None], new_anchor, new_momentum)


def solution(mesh):
    fine = Mesh(mesh.devices.reshape(2, 4, 2, 4, 4), ("zh", "y", "c", "zl", "x"))
    replica, fsdp = ("zh", "y", "c"), ("zl", "x")
    tokens, stacked, shared = P(replica + fsdp, None), P(replica, fsdp, None), P(fsdp, None)
    return jax.shard_map(
        on_device,
        mesh=fine,
        in_specs=(tokens, tokens, stacked, stacked, stacked, stacked, shared, shared),
        out_specs=(tokens, stacked, stacked, stacked, shared, shared),
        check_vma=False,
    )
```

```python
import jax
import jax.numpy as jnp
from jax import lax
from jax.experimental import pallas as pl
from jax.experimental.pallas import tpu as pltpu
from jax.sharding import Mesh, PartitionSpec as P

learn_rate = 0.001
weight_decay = 0.1
first_decay = 0.9
second_decay = 0.95
adam_floor = 1e-08
outer_rate = 0.7
outer_decay = 0.9

bf16, f32 = jnp.bfloat16, jnp.float32

HOME = (0, 1, 1, 0)
SWAP = [(c * 4 + x, (1 - c) * 4 + (x ^ 1)) for c in range(2) for x in range(4) if c != HOME[x]]
CORE = [(0, 1), (1, 0)]
ACROSS = [(x, 3 - x) for x in range(4)]
BESIDE = [(x, x ^ 1) for x in range(4)]
ENDS_OUT = [(1, 0), (2, 3)]
PAIRS = [(0, 1), (1, 0), (2, 3), (3, 2)]
MIDDLE = [(1, 2), (2, 1)]
ORDER = ((3, 2, 1, 0), (3, 2, 0, 1), (0, 1, 3, 2), (0, 1, 2, 3))


def swap(v):
    return lax.ppermute(v, ("c", "x"), SWAP)


def core(v):
    return lax.ppermute(v, "c", CORE)


def beside(v):
    return lax.ppermute(v, "x", BESIDE)


def across(v):
    return lax.ppermute(v, "x", ACROSS)


def line(v, pairs):
    return lax.ppermute(v, "zl", pairs)


def dot(a, b):
    return jnp.dot(a, b, preferred_element_type=f32)


def dot_t(a, b):
    return lax.dot_general(a, b, (((0,), (0,)), ((), ())), preferred_element_type=f32)


def together(*arrays):
    return lax.optimization_barrier(arrays)


def after(array, *earlier):
    return together(array, *earlier)[0]


def move(_, a, b, to_a, to_b):
    to_a[0] = a[...]
    to_b[0] = b[...]


def halves(tokens, blocks):
    spec = lambda i: pl.BlockSpec((512, 256), lambda n, table: (0, table[i, n]))
    out = pl.BlockSpec((1, 512, 256), lambda n, table: (n // 2, 0, n % 2))
    steps = blocks.shape[1]
    kind = jax.ShapeDtypeStruct((steps // 2, 512, 512), bf16)
    return pl.pallas_call(
        move,
        grid_spec=pltpu.PrefetchScalarGridSpec(
            num_scalar_prefetch=1,
            grid=(steps,),
            in_specs=[spec(0), spec(1)],
            out_specs=[out, out],
        ),
        out_shape=[kind, kind],
        cost_estimate=pl.CostEstimate(flops=0, bytes_accessed=0, transcendentals=0),
    )(blocks, tokens, tokens)


class Drift:
    def __init__(self, own, c, y):
        near = [(i, i ^ 1) for i in range(4)]
        wide = [(i, i ^ 2) for i in range(4)]
        self.v = own
        self.steps = [("c", CORE, c), ("y", near, y % 2), ("y", wide, y // 2), ("zh", CORE, c)]
        self.at = 0

    def send(self):
        if self.at < 3:
            bit = self.steps[self.at][2]
            n = self.v.shape[0] // 2
            self.sent = lax.dynamic_slice_in_dim(self.v, (1 - bit) * n, n, 0)
        elif self.at == 3:
            (self.sent,) = together(self.v.astype(bf16))
        else:
            self.sent = self.v
        axis, perm, _ = self.steps[min(self.at, 6 - self.at)]
        return lax.ppermute(self.sent, axis, perm)

    def take(self, got):
        bit = self.steps[min(self.at, 6 - self.at)][2]
        v = self.v
        if self.at < 3:
            n = v.shape[0] // 2
            self.v = lax.dynamic_slice_in_dim(v, bit * n, n, 0) + got
        elif self.at == 3:
            self.v = self.sent.astype(f32) + got.astype(f32)
        else:
            self.v = jnp.where(bit == 0, jnp.concatenate([v, got]), jnp.concatenate([got, v]))
        self.at += 1


def on_device(
    tokens, key_grad, key_weight, adam_first, adam_second, local_params, anchor, outer_momentum
):
    c, x, z, y = (lax.axis_index(a) for a in ("c", "x", "zl", "y"))
    weight = key_weight[0]
    stays = c == jnp.where((x == 1) | (x == 2), 1, 0)
    end = (z == 0) | (z == 3)
    mine = jnp.where(x < 2, c, 3 - c)
    theirs = jnp.where(x < 2, 1 - c, 2 + c)
    order = [
        jnp.where(z < 2, 3, 0),
        jnp.where(z < 2, 2, 1),
        jnp.where(z == 0, 1, jnp.where(z == 1, 0, jnp.where(z == 2, 3, 2))),
        z,
    ]
    blocks = jnp.stack(
        [4 * order[k] + q for half in (theirs, mine) for k in range(4) for q in (half, 3 - half)]
    ).reshape(2, 8)

    w = swap(weight)
    g_mine = lax.dynamic_slice_in_dim(key_grad, c * 256, 256, 0)
    g_first = core(lax.dynamic_slice_in_dim(key_grad, (1 - c) * 256, 256, 0))
    g_l = jnp.where(stays, g_first, g_mine)
    g_half0 = beside(g_l[:128])
    blocks = blocks.astype(jnp.int32)
    w, g_half0, blocks = together(w, g_half0, blocks)
    w = jnp.where(stays, weight, w)
    drift = Drift(after(anchor - local_params[0].astype(f32), g_l), c, y)
    drift.take(drift.send())

    give0, own0 = halves(tokens, blocks[:, :2])
    sib0 = core(give0)
    give, own = halves(tokens, after(blocks[:, 2:], sib0))
    drift.take(drift.send())
    got = (beside(g_l[128:]), line(w, PAIRS), line(w, MIDDLE), across(w), drift.send())
    leave = [jnp.where(stays, sib0[0], own0[0])]
    keep = [jnp.where(stays, own0[0], sib0[0])]
    sib = core(give)
    got, leave, sib, own, g_mine, drift.v = together(got, leave, sib, own, g_mine, drift.v)
    g_half, e_own, m_own, q_own, d = got
    g_half = jnp.concatenate([g_half0, g_half])
    drift.take(d)

    got = (beside(leave[0]), line(m_own, ENDS_OUT), line(e_own, MIDDLE), across(e_own))
    leave += [jnp.where(stays, sib[k], own[k]) for k in range(3)]
    keep += [jnp.where(stays, own[k], sib[k]) for k in range(3)]
    rest = core(jnp.concatenate([g_half, g_mine]))

    def in_order(a, b):
        return jnp.where(c == 0, jnp.concatenate([a, b]), jnp.concatenate([b, a]))

    g_b = in_order(g_half, rest[:256])
    g_a = jnp.where(stays, key_grad, in_order(g_first, rest[256:]))
    base = [dot_t(k, g_a) for k in keep]
    drift.v = after(drift.v, g_b)
    got += (drift.send(),)
    got, leave, drift.sent, g_b, base = together(got, leave, drift.sent, g_b, base)
    x_b = [got[0]]
    _, e2, m2, q2, d = got
    drift.take(d)
    mid = jnp.where(end, e2, m_own)

    def going(k):
        return (base[k][256:] + dot_t(x_b[k][:, 256:], g_b)).astype(bf16)

    def staying(k):
        return base[k][:256] + dot_t(x_b[k][:, :256], g_b)

    def cat(*arrays):
        return jnp.concatenate(arrays, axis=-1)

    got = (beside(leave[1]), line(m2, ENDS_OUT), line(q_own, MIDDLE), across(going(0)), drift.send())
    rows = [None, None, jnp.concatenate([e_own, q2]), jnp.concatenate([w, q_own])]
    k_a = dot(cat(keep[2], keep[3]), jnp.concatenate(rows[2:]))
    stay = staying(0)
    got, leave, drift.v, stay, k_a = together(got, leave, drift.v, stay, k_a)
    x_b.append(got[0])
    _, e3, m3, q3, d = got
    drift.take(d)
    part0 = stay + q3.astype(f32)

    got = (
        beside(leave[2]),
        line(jnp.where(end, part0.astype(bf16), m3), PAIRS),
        line(q2, MIDDLE),
        across(going(1)),
        drift.send(),
    )
    stay = staying(1)
    got, leave, drift.v, stay, part0 = together(got, leave, drift.v, stay, part0)
    x_b.append(got[0])
    _, e4, m4, q4, d = got
    drift.take(d)
    part1 = stay + q4.astype(f32)

    got = (
        beside(leave[3]),
        line(jnp.where(end, part1.astype(bf16), m4), PAIRS),
        line((part0 + e4.astype(f32)).astype(bf16), MIDDLE),
        across(going(2)),
        drift.send(),
    )
    rows[1] = jnp.concatenate([mid, jnp.where(end, e4, m3)])
    k_a = k_a + dot(keep[1], rows[1])
    k_b = dot(cat(x_b[1], x_b[2]), jnp.concatenate(rows[1:3]))
    stay = staying(2)
    got, drift.v, stay, part1, k_a, k_b = together(got, drift.v, stay, part1, k_a, k_b)
    x_b.append(got[0])
    _, e5, m5, q5, d = got
    drift.take(d)
    part2 = stay + q5.astype(f32)

    got = (
        line((part2 + m5.astype(f32)).astype(bf16), PAIRS),
        line((part1 + e5.astype(f32)).astype(bf16), MIDDLE),
        across(going(3)),
    )
    rows[0] = jnp.concatenate([jnp.where(end, e3, m2), jnp.where(end, e5, m4)])
    k_a = k_a + dot(keep[0], rows[0])
    k_b = k_b + dot(cat(x_b[0], x_b[3]), jnp.concatenate([rows[0], rows[3]]))
    k_got = core(jnp.where(stays, k_b, k_a).astype(bf16))
    keys_work = (jnp.where(stays, k_a, k_b) + k_got.astype(f32)).astype(bf16)
    keys = jnp.where(stays, keys_work, swap(keys_work))
    e6, m6, q6 = got
    total = staying(3) + q6.astype(f32) + e6.astype(f32) + m6.astype(f32)
    gradient = jnp.where(stays, total, swap(total.astype(bf16)).astype(f32))
    new_first = first_decay * adam_first[0] + (1.0 - first_decay) * gradient
    new_second = second_decay * adam_second[0] + (1.0 - second_decay) * gradient * gradient
    master = weight.astype(f32)
    update = new_first / (jnp.sqrt(new_second) + adam_floor) + weight_decay * master
    new_weight = (master - learn_rate * update).astype(bf16)

    mean = drift.v / 16
    new_momentum = outer_decay * outer_momentum + mean
    new_anchor = anchor - outer_rate * (mean + outer_decay * new_momentum)
    return (keys, new_weight[None], new_first[None], new_second[None], new_anchor, new_momentum)


def solution(mesh):
    fine = Mesh(mesh.devices.reshape(2, 4, 2, 4, 4), ("zh", "y", "c", "zl", "x"))
    replica, fsdp = ("zh", "y", "c"), ("zl", "x")
    tokens, stacked, shared = P(replica + fsdp, None), P(replica, fsdp, None), P(fsdp, None)
    return jax.shard_map(
        on_device,
        mesh=fine,
        in_specs=(tokens, tokens, stacked, stacked, stacked, stacked, shared, shared),
        out_specs=(tokens, stacked, stacked, stacked, shared, shared),
        check_vma=False,
    )
```

```python
import jax
import jax.numpy as jnp
from jax import lax
from jax.experimental import pallas as pl
from jax.experimental.pallas import tpu as pltpu
from jax.sharding import Mesh, PartitionSpec as P

learn_rate = 0.001
weight_decay = 0.1
first_decay = 0.9
second_decay = 0.95
adam_floor = 1e-08
outer_rate = 0.7
outer_decay = 0.9

bf16, f32 = jnp.bfloat16, jnp.float32

HOME = (0, 1, 1, 0)
SWAP = [(c * 4 + x, (1 - c) * 4 + (x ^ 1)) for c in range(2) for x in range(4) if c != HOME[x]]
CORE = [(0, 1), (1, 0)]
ACROSS = [(x, 3 - x) for x in range(4)]
BESIDE = [(x, x ^ 1) for x in range(4)]
ENDS_OUT = [(1, 0), (2, 3)]
PAIRS = [(0, 1), (1, 0), (2, 3), (3, 2)]
MIDDLE = [(1, 2), (2, 1)]
ORDER = ((3, 2, 1, 0), (3, 2, 0, 1), (0, 1, 3, 2), (0, 1, 2, 3))


def swap(v):
    return lax.ppermute(v, ("c", "x"), SWAP)


def core(v):
    return lax.ppermute(v, "c", CORE)


def beside(v):
    return lax.ppermute(v, "x", BESIDE)


def across(v):
    return lax.ppermute(v, "x", ACROSS)


def line(v, pairs):
    return lax.ppermute(v, "zl", pairs)


def dot(a, b):
    return jnp.dot(a, b, preferred_element_type=f32)


def dot_t(a, b):
    return lax.dot_general(a, b, (((0,), (0,)), ((), ())), preferred_element_type=f32)


def together(*arrays):
    return lax.optimization_barrier(arrays)


def move(_, a0, a1, b0, b1, to_a, to_b):
    to_a[0, :, :256] = a0[...]
    to_a[0, :, 256:] = a1[...]
    to_b[0, :, :256] = b0[...]
    to_b[0, :, 256:] = b1[...]


def halves(tokens, blocks):
    def spec(half, place):
        return pl.BlockSpec((512, 256), lambda n, table: (0, table[half, 2 * n + place]))

    out = pl.BlockSpec((1, 512, 512), lambda n, table: (n, 0, 0))
    kind = jax.ShapeDtypeStruct((4, 512, 512), bf16)
    return pl.pallas_call(
        move,
        grid_spec=pltpu.PrefetchScalarGridSpec(
            num_scalar_prefetch=1,
            grid=(4,),
            in_specs=[spec(half, place) for half in range(2) for place in range(2)],
            out_specs=[out, out],
        ),
        out_shape=[kind, kind],
        cost_estimate=pl.CostEstimate(flops=0, bytes_accessed=16 << 20, transcendentals=0),
    )(blocks, tokens, tokens, tokens, tokens)


class Drift:
    def __init__(self, own, c, y):
        near = [(i, i ^ 1) for i in range(4)]
        wide = [(i, i ^ 2) for i in range(4)]
        self.v = own
        self.steps = [("c", CORE, c), ("y", near, y % 2), ("y", wide, y // 2), ("zh", CORE, c)]
        self.at = 0

    def send(self, earlier=None):
        if earlier is not None:
            self.v, _ = together(self.v, earlier)
        if self.at < 3:
            bit = self.steps[self.at][2]
            n = self.v.shape[0] // 2
            self.sent = lax.dynamic_slice_in_dim(self.v, (1 - bit) * n, n, 0)
        elif self.at == 3:
            (self.sent,) = together(self.v.astype(bf16))
        else:
            self.sent = self.v
        axis, perm, _ = self.steps[min(self.at, 6 - self.at)]
        return lax.ppermute(self.sent, axis, perm)

    def take(self, got):
        bit = self.steps[min(self.at, 6 - self.at)][2]
        v = self.v
        if self.at < 3:
            n = v.shape[0] // 2
            self.v = lax.dynamic_slice_in_dim(v, bit * n, n, 0) + got
        elif self.at == 3:
            self.v = self.sent.astype(f32) + got.astype(f32)
        else:
            self.v = jnp.where(bit == 0, jnp.concatenate([v, got]), jnp.concatenate([got, v]))
        self.at += 1


def on_device(
    tokens, key_grad, key_weight, adam_first, adam_second, local_params, anchor, outer_momentum
):
    c, x, z, y = (lax.axis_index(a) for a in ("c", "x", "zl", "y"))
    weight = key_weight[0]
    stays = c == jnp.where((x == 1) | (x == 2), 1, 0)
    end = (z == 0) | (z == 3)
    mine = jnp.where(x < 2, c, 3 - c)
    theirs = jnp.where(x < 2, 1 - c, 2 + c)
    order = [
        jnp.where(z < 2, 3, 0),
        jnp.where(z < 2, 2, 1),
        jnp.where(z == 0, 1, jnp.where(z == 1, 0, jnp.where(z == 2, 3, 2))),
        z,
    ]
    blocks = jnp.stack(
        [4 * order[k] + q for half in (theirs, mine) for k in range(4) for q in (half, 3 - half)]
    ).reshape(2, 8)

    w = jnp.where(stays, weight, swap(weight))
    g_sib = core(key_grad)
    x_give, x_own = halves(tokens, blocks.astype(jnp.int32))
    x_sib = core(x_give)
    drift = Drift(anchor - local_params[0].astype(f32), c, y)
    drift.take(drift.send())
    g_a = jnp.where(stays, key_grad, g_sib)
    g_l = lax.dynamic_slice_in_dim(jnp.where(stays, g_sib, key_grad), c * 256, 256, 0)

    got = (beside(g_l), line(w, PAIRS), line(w, MIDDLE), across(w), drift.send())
    leave = [jnp.where(stays, x_sib[k], x_own[k]) for k in range(4)]
    keep = [jnp.where(stays, x_own[k], x_sib[k]) for k in range(4)]
    got, leave, drift.v = together(got, leave, drift.v)
    g_half, e_own, m_own, q_own, d = got
    drift.take(d)

    got = (beside(leave[0]), line(m_own, ENDS_OUT), line(e_own, MIDDLE), across(e_own), drift.send())
    g_rest = core(g_half)
    g_b = jnp.where(
        c == 0, jnp.concatenate([g_half, g_rest]), jnp.concatenate([g_rest, g_half])
    )
    base = [dot_t(k, g_a) for k in keep]
    sent = drift.v
    got, leave, sent, g_b, base = together(got, leave, sent, g_b, base)
    drift.v = sent
    x_b = [got[0]]
    _, e2, m2, q2, d = got
    drift.take(d)
    mid = jnp.where(end, e2, m_own)

    def going(k):
        return (base[k][256:] + dot_t(x_b[k][:, 256:], g_b)).astype(bf16)

    def staying(k):
        return base[k][:256] + dot_t(x_b[k][:, :256], g_b)

    def cat(*arrays):
        return jnp.concatenate(arrays, axis=-1)

    m3 = line(q_own, MIDDLE)
    got = (beside(leave[1]), line(m2, ENDS_OUT), m3, across(going(0)), drift.send(m3))
    rows = [None, None, jnp.concatenate([e_own, q2]), jnp.concatenate([w, q_own])]
    k_a = dot(cat(keep[2], keep[3]), jnp.concatenate(rows[2:]))
    stay = staying(0)
    got, leave, drift.v, drift.sent, stay, k_a = together(got, leave, drift.v, drift.sent, stay, k_a)
    x_b.append(got[0])
    _, e3, m3, q3, d = got
    drift.take(d)
    part0 = stay + q3.astype(f32)

    m4 = line(q2, MIDDLE)
    got = (
        beside(leave[2]),
        line(jnp.where(end, part0.astype(bf16), m3), PAIRS),
        m4,
        across(going(1)),
        drift.send(m4),
    )
    stay = staying(1)
    got, leave, drift.v, stay, part0 = together(got, leave, drift.v, stay, part0)
    x_b.append(got[0])
    _, e4, m4, q4, d = got
    drift.take(d)
    part1 = stay + q4.astype(f32)

    got = (
        beside(leave[3]),
        line(jnp.where(end, part1.astype(bf16), m4), PAIRS),
        line((part0 + e4.astype(f32)).astype(bf16), MIDDLE),
        across(going(2)),
        drift.send(),
    )
    rows[1] = jnp.concatenate([mid, jnp.where(end, e4, m3)])
    k_a = k_a + dot(keep[1], rows[1])
    k_b = dot(cat(x_b[1], x_b[2]), jnp.concatenate(rows[1:3]))
    stay = staying(2)
    got, drift.v, stay, part1, k_a, k_b = together(got, drift.v, stay, part1, k_a, k_b)
    x_b.append(got[0])
    _, e5, m5, q5, d = got
    drift.take(d)
    part2 = stay + q5.astype(f32)

    got = (
        line((part2 + m5.astype(f32)).astype(bf16), PAIRS),
        line((part1 + e5.astype(f32)).astype(bf16), MIDDLE),
        across(going(3)),
    )
    rows[0] = jnp.concatenate([jnp.where(end, e3, m2), jnp.where(end, e5, m4)])
    k_a = k_a + dot(keep[0], rows[0])
    k_b = k_b + dot(cat(x_b[0], x_b[3]), jnp.concatenate([rows[0], rows[3]]))
    k_got = core(jnp.where(stays, k_b, k_a).astype(bf16))
    keys_work = (jnp.where(stays, k_a, k_b) + k_got.astype(f32)).astype(bf16)
    keys = jnp.where(stays, keys_work, swap(keys_work))
    e6, m6, q6 = got
    total = staying(3) + q6.astype(f32) + e6.astype(f32) + m6.astype(f32)
    back, keys = together(swap(total.astype(bf16)), keys)
    gradient = jnp.where(stays, total, back.astype(f32))
    drift.take(drift.send())

    new_first = first_decay * adam_first[0] + (1.0 - first_decay) * gradient
    new_second = second_decay * adam_second[0] + (1.0 - second_decay) * gradient * gradient
    master = weight.astype(f32)
    update = new_first / (jnp.sqrt(new_second) + adam_floor) + weight_decay * master
    new_weight = (master - learn_rate * update).astype(bf16)

    mean = drift.v / 16
    new_momentum = outer_decay * outer_momentum + mean
    new_anchor = anchor - outer_rate * (mean + outer_decay * new_momentum)
    return (keys, new_weight[None], new_first[None], new_second[None], new_anchor, new_momentum)


def solution(mesh):
    fine = Mesh(mesh.devices.reshape(2, 4, 2, 4, 4), ("zh", "y", "c", "zl", "x"))
    replica, fsdp = ("zh", "y", "c"), ("zl", "x")
    tokens, stacked, shared = P(replica + fsdp, None), P(replica, fsdp, None), P(fsdp, None)
    return jax.shard_map(
        on_device,
        mesh=fine,
        in_specs=(tokens, tokens, stacked, stacked, stacked, stacked, shared, shared),
        out_specs=(tokens, stacked, stacked, stacked, shared, shared),
        check_vma=False,
    )
```

```python
import jax
import jax.numpy as jnp
from jax import lax
from jax.experimental import pallas as pl
from jax.experimental.pallas import tpu as pltpu
from jax.sharding import Mesh, PartitionSpec as P

learn_rate = 0.001
weight_decay = 0.1
first_decay = 0.9
second_decay = 0.95
adam_floor = 1e-08
outer_rate = 0.7
outer_decay = 0.9

bf16, f32 = jnp.bfloat16, jnp.float32

HOME = (0, 1, 1, 0)
SWAP = [(c * 4 + x, (1 - c) * 4 + (x ^ 1)) for c in range(2) for x in range(4) if c != HOME[x]]
CORE = [(0, 1), (1, 0)]
ACROSS = [(x, 3 - x) for x in range(4)]
BESIDE = [(x, x ^ 1) for x in range(4)]
ENDS_OUT = [(1, 0), (2, 3)]
PAIRS = [(0, 1), (1, 0), (2, 3), (3, 2)]
MIDDLE = [(1, 2), (2, 1)]
ORDER = ((3, 2, 1, 0), (3, 2, 0, 1), (0, 1, 3, 2), (0, 1, 2, 3))


def swap(v):
    return lax.ppermute(v, ("c", "x"), SWAP)


def core(v):
    return lax.ppermute(v, "c", CORE)


def beside(v):
    return lax.ppermute(v, "x", BESIDE)


def across(v):
    return lax.ppermute(v, "x", ACROSS)


def line(v, pairs):
    return lax.ppermute(v, "zl", pairs)


def dot(a, b):
    return jnp.dot(a, b, preferred_element_type=f32)


def dot_t(a, b):
    return lax.dot_general(a, b, (((0,), (0,)), ((), ())), preferred_element_type=f32)


def together(*arrays):
    return lax.optimization_barrier(arrays)


def after(array, *earlier):
    return together(array, *earlier)[0]


def move(_, a, b, to_a, to_b):
    to_a[0] = a[...]
    to_b[0] = b[...]


def halves(tokens, blocks):
    spec = lambda i: pl.BlockSpec((512, 256), lambda n, table: (0, table[i, n]))
    out = pl.BlockSpec((1, 512, 256), lambda n, table: (n // 2, 0, n % 2))
    kind = jax.ShapeDtypeStruct((4, 512, 512), bf16)
    return pl.pallas_call(
        move,
        grid_spec=pltpu.PrefetchScalarGridSpec(
            num_scalar_prefetch=1,
            grid=(8,),
            in_specs=[spec(0), spec(1)],
            out_specs=[out, out],
        ),
        out_shape=[kind, kind],
        cost_estimate=pl.CostEstimate(flops=0, bytes_accessed=16 << 20, transcendentals=0),
    )(blocks, tokens, tokens)


class Drift:
    def __init__(self, own, c, y):
        near = [(i, i ^ 1) for i in range(4)]
        wide = [(i, i ^ 2) for i in range(4)]
        self.v = own
        self.steps = [("c", CORE, c), ("y", near, y % 2), ("y", wide, y // 2), ("zh", CORE, c)]
        self.at = 0

    def send(self, *earlier):
        self.v = after(self.v, *earlier)
        if self.at < 3:
            bit = self.steps[self.at][2]
            n = self.v.shape[0] // 2
            self.sent = lax.dynamic_slice_in_dim(self.v, (1 - bit) * n, n, 0)
        elif self.at == 3:
            (self.sent,) = together(self.v.astype(bf16))
        else:
            self.sent = self.v
        axis, perm, _ = self.steps[min(self.at, 6 - self.at)]
        return lax.ppermute(self.sent, axis, perm)

    def take(self, got):
        bit = self.steps[min(self.at, 6 - self.at)][2]
        v = self.v
        if self.at < 3:
            n = v.shape[0] // 2
            self.v = lax.dynamic_slice_in_dim(v, bit * n, n, 0) + got
        elif self.at == 3:
            self.v = self.sent.astype(f32) + got.astype(f32)
        else:
            self.v = jnp.where(bit == 0, jnp.concatenate([v, got]), jnp.concatenate([got, v]))
        self.at += 1


def on_device(
    tokens, key_grad, key_weight, adam_first, adam_second, local_params, anchor, outer_momentum
):
    c, x, z, y = (lax.axis_index(a) for a in ("c", "x", "zl", "y"))
    weight = key_weight[0]
    stays = c == jnp.where((x == 1) | (x == 2), 1, 0)
    end = (z == 0) | (z == 3)
    mine = jnp.where(x < 2, c, 3 - c)
    theirs = jnp.where(x < 2, 1 - c, 2 + c)
    order = [
        jnp.where(z < 2, 3, 0),
        jnp.where(z < 2, 2, 1),
        jnp.where(z == 0, 1, jnp.where(z == 1, 0, jnp.where(z == 2, 3, 2))),
        z,
    ]
    blocks = jnp.stack(
        [4 * order[k] + q for half in (theirs, mine) for k in range(4) for q in (half, 3 - half)]
    ).reshape(2, 8)

    w = jnp.where(stays, weight, swap(weight))
    g_sib = core(key_grad)
    x_give, x_own = halves(tokens, blocks.astype(jnp.int32))
    x_sib = core(x_give)
    drift = Drift(anchor - local_params[0].astype(f32), c, y)
    drift.take(drift.send())
    g_a = jnp.where(stays, key_grad, g_sib)
    g_l = lax.dynamic_slice_in_dim(jnp.where(stays, g_sib, key_grad), c * 256, 256, 0)

    got = (beside(g_l), line(w, PAIRS), line(w, MIDDLE), across(w), drift.send())
    leave = [jnp.where(stays, x_sib[k], x_own[k]) for k in range(4)]
    keep = [jnp.where(stays, x_own[k], x_sib[k]) for k in range(4)]
    got, leave, drift.v = together(got, leave, drift.v)
    g_half, e_own, m_own, q_own, d = got
    drift.take(d)

    x_b = [beside(leave[0])]
    e2, m2, q2 = line(m_own, ENDS_OUT), line(e_own, MIDDLE), across(e_own)
    drift.take(drift.send(m2))
    g_rest = core(g_half)
    g_b = jnp.where(
        c == 0, jnp.concatenate([g_half, g_rest]), jnp.concatenate([g_rest, g_half])
    )
    base = [dot_t(k, g_a) for k in keep]
    mid = jnp.where(end, e2, m_own)

    def going(k):
        return (base[k][256:] + dot_t(x_b[k][:, 256:], g_b)).astype(bf16)

    def staying(k):
        return base[k][:256] + dot_t(x_b[k][:, :256], g_b)

    def cat(*arrays):
        return jnp.concatenate(arrays, axis=-1)

    x_b.append(beside(after(leave[1], x_b[0])))
    e3 = line(after(m2, e2, x_b[0]), ENDS_OUT)
    m3 = line(after(q_own, m2, x_b[0]), MIDDLE)
    q3 = across(after(going(0), q2))
    drift.take(drift.send(m3))
    rows = [None, None, jnp.concatenate([e_own, q2]), jnp.concatenate([w, q_own])]
    k_a = dot(cat(keep[2], keep[3]), jnp.concatenate(rows[2:]))
    part0 = staying(0) + q3.astype(f32)

    x_b.append(beside(after(leave[2], x_b[1])))
    e4 = line(after(jnp.where(end, part0.astype(bf16), m3), e3, x_b[1]), PAIRS)
    m4 = line(after(q2, m3, x_b[1]), MIDDLE)
    q4 = across(after(going(1), q3))
    drift.take(drift.send(m4))
    part1 = staying(1) + q4.astype(f32)

    x_b.append(beside(after(leave[3], x_b[2])))
    e5 = line(after(jnp.where(end, part1.astype(bf16), m4), e4, x_b[2]), PAIRS)
    m5 = line(after((part0 + e4.astype(f32)).astype(bf16), m4, x_b[2]), MIDDLE)
    q5 = across(after(going(2), q4))
    drift.take(drift.send(q4))
    rows[1] = jnp.concatenate([mid, jnp.where(end, e4, m3)])
    k_a = k_a + dot(keep[1], rows[1])
    k_b = dot(cat(x_b[1], x_b[2]), jnp.concatenate(rows[1:3]))
    part2 = staying(2) + q5.astype(f32)
    (x_b[3], e5, m5, q5), drift.v, part1, part2, k_a, k_b = together(
        (x_b[3], e5, m5, q5), drift.v, part1, part2, k_a, k_b
    )

    got = (
        line((part2 + m5.astype(f32)).astype(bf16), PAIRS),
        line((part1 + e5.astype(f32)).astype(bf16), MIDDLE),
        across(going(3)),
    )
    rows[0] = jnp.concatenate([jnp.where(end, e3, m2), jnp.where(end, e5, m4)])
    k_a = k_a + dot(keep[0], rows[0])
    k_b = k_b + dot(cat(x_b[0], x_b[3]), jnp.concatenate([rows[0], rows[3]]))
    k_got = core(jnp.where(stays, k_b, k_a).astype(bf16))
    keys_work = (jnp.where(stays, k_a, k_b) + k_got.astype(f32)).astype(bf16)
    keys = jnp.where(stays, keys_work, swap(keys_work))
    e6, m6, q6 = got
    total = staying(3) + q6.astype(f32) + e6.astype(f32) + m6.astype(f32)
    gradient = jnp.where(stays, total, swap(total.astype(bf16)).astype(f32))
    drift.take(drift.send())

    new_first = first_decay * adam_first[0] + (1.0 - first_decay) * gradient
    new_second = second_decay * adam_second[0] + (1.0 - second_decay) * gradient * gradient
    master = weight.astype(f32)
    update = new_first / (jnp.sqrt(new_second) + adam_floor) + weight_decay * master
    new_weight = (master - learn_rate * update).astype(bf16)

    mean = drift.v / 16
    new_momentum = outer_decay * outer_momentum + mean
    new_anchor = anchor - outer_rate * (mean + outer_decay * new_momentum)
    return (keys, new_weight[None], new_first[None], new_second[None], new_anchor, new_momentum)


def solution(mesh):
    fine = Mesh(mesh.devices.reshape(2, 4, 2, 4, 4), ("zh", "y", "c", "zl", "x"))
    replica, fsdp = ("zh", "y", "c"), ("zl", "x")
    tokens, stacked, shared = P(replica + fsdp, None), P(replica, fsdp, None), P(fsdp, None)
    return jax.shard_map(
        on_device,
        mesh=fine,
        in_specs=(tokens, tokens, stacked, stacked, stacked, stacked, shared, shared),
        out_specs=(tokens, stacked, stacked, stacked, shared, shared),
        check_vma=False,
    )
```

```python
import jax
import jax.numpy as jnp
from jax import lax
from jax.experimental import pallas as pl
from jax.experimental.pallas import tpu as pltpu
from jax.sharding import Mesh, PartitionSpec as P

learn_rate = 0.001
weight_decay = 0.1
first_decay = 0.9
second_decay = 0.95
adam_floor = 1e-08
outer_rate = 0.7
outer_decay = 0.9

bf16, f32 = jnp.bfloat16, jnp.float32

HOME = (0, 1, 1, 0)
SWAP = [(c * 4 + x, (1 - c) * 4 + (x ^ 1)) for c in range(2) for x in range(4) if c != HOME[x]]
CORE = [(0, 1), (1, 0)]
ACROSS = [(x, 3 - x) for x in range(4)]
BESIDE = [(x, x ^ 1) for x in range(4)]
ENDS_OUT = [(1, 0), (2, 3)]
PAIRS = [(0, 1), (1, 0), (2, 3), (3, 2)]
MIDDLE = [(1, 2), (2, 1)]
ORDER = ((3, 2, 1, 0), (3, 2, 0, 1), (0, 1, 3, 2), (0, 1, 2, 3))


def swap(v):
    return lax.ppermute(v, ("c", "x"), SWAP)


def core(v):
    return lax.ppermute(v, "c", CORE)


def beside(v):
    return lax.ppermute(v, "x", BESIDE)


def across(v):
    return lax.ppermute(v, "x", ACROSS)


def line(v, pairs):
    return lax.ppermute(v, "zl", pairs)


def dot(a, b):
    return jnp.dot(a, b, preferred_element_type=f32)


def dot_t(a, b):
    return lax.dot_general(a, b, (((0,), (0,)), ((), ())), preferred_element_type=f32)


def together(*arrays):
    return lax.optimization_barrier(arrays)


def after(array, *earlier):
    return together(array, *earlier)[0]


def move(_, a0, a1, b0, b1, to_a, to_b):
    to_a[0, :, :256] = a0[...]
    to_a[0, :, 256:] = a1[...]
    to_b[0, :, :256] = b0[...]
    to_b[0, :, 256:] = b1[...]


def halves(tokens, blocks):
    def spec(half, place):
        return pl.BlockSpec((512, 256), lambda n, table: (0, table[half, 2 * n + place]))

    out = pl.BlockSpec((1, 512, 512), lambda n, table: (n, 0, 0))
    kind = jax.ShapeDtypeStruct((4, 512, 512), bf16)
    return pl.pallas_call(
        move,
        grid_spec=pltpu.PrefetchScalarGridSpec(
            num_scalar_prefetch=1,
            grid=(4,),
            in_specs=[spec(half, place) for half in range(2) for place in range(2)],
            out_specs=[out, out],
        ),
        out_shape=[kind, kind],
        cost_estimate=pl.CostEstimate(flops=0, bytes_accessed=16 << 20, transcendentals=0),
    )(blocks, tokens, tokens, tokens, tokens)


class Drift:
    def __init__(self, own, c, y):
        near = [(i, i ^ 1) for i in range(4)]
        wide = [(i, i ^ 2) for i in range(4)]
        self.v = own
        self.steps = [("c", CORE, c), ("y", near, y % 2), ("y", wide, y // 2), ("zh", CORE, c)]
        self.at = 0

    def send(self, *earlier):
        self.v = after(self.v, *earlier)
        if self.at < 3:
            bit = self.steps[self.at][2]
            n = self.v.shape[0] // 2
            self.sent = lax.dynamic_slice_in_dim(self.v, (1 - bit) * n, n, 0)
        elif self.at == 3:
            (self.sent,) = together(self.v.astype(bf16))
        else:
            self.sent = self.v
        axis, perm, _ = self.steps[min(self.at, 6 - self.at)]
        return lax.ppermute(self.sent, axis, perm)

    def take(self, got):
        bit = self.steps[min(self.at, 6 - self.at)][2]
        v = self.v
        if self.at < 3:
            n = v.shape[0] // 2
            self.v = lax.dynamic_slice_in_dim(v, bit * n, n, 0) + got
        elif self.at == 3:
            self.v = self.sent.astype(f32) + got.astype(f32)
        else:
            self.v = jnp.where(bit == 0, jnp.concatenate([v, got]), jnp.concatenate([got, v]))
        self.at += 1


def on_device(
    tokens, key_grad, key_weight, adam_first, adam_second, local_params, anchor, outer_momentum
):
    c, x, z, y = (lax.axis_index(a) for a in ("c", "x", "zl", "y"))
    weight = key_weight[0]
    stays = c == jnp.where((x == 1) | (x == 2), 1, 0)
    end = (z == 0) | (z == 3)
    mine = jnp.where(x < 2, c, 3 - c)
    theirs = jnp.where(x < 2, 1 - c, 2 + c)
    order = [
        jnp.where(z < 2, 3, 0),
        jnp.where(z < 2, 2, 1),
        jnp.where(z == 0, 1, jnp.where(z == 1, 0, jnp.where(z == 2, 3, 2))),
        z,
    ]
    blocks = jnp.stack(
        [4 * order[k] + q for half in (theirs, mine) for k in range(4) for q in (half, 3 - half)]
    ).reshape(2, 8)

    drift = Drift(anchor - local_params[0].astype(f32), c, y)
    w, g_sib, d, blocks, drift.v = together(
        swap(weight), core(key_grad), drift.send(), blocks.astype(jnp.int32), drift.v
    )
    drift.take(d)
    w = jnp.where(stays, weight, w)
    g_a = jnp.where(stays, key_grad, g_sib)
    g_l = lax.dynamic_slice_in_dim(jnp.where(stays, g_sib, key_grad), c * 256, 256, 0)
    x_give, x_own = halves(tokens, blocks)
    x_sib = core(x_give)

    got = (beside(g_l), line(w, PAIRS), line(w, MIDDLE), across(w), drift.send())
    leave = [jnp.where(stays, x_sib[k], x_own[k]) for k in range(4)]
    keep = [jnp.where(stays, x_own[k], x_sib[k]) for k in range(4)]
    got, leave, drift.v = together(got, leave, drift.v)
    g_half, e_own, m_own, q_own, d = got
    drift.take(d)

    x_b = [beside(leave[0])]
    e2, m2, q2 = line(m_own, ENDS_OUT), line(e_own, MIDDLE), across(e_own)
    drift.take(drift.send(m2))
    g_rest = core(g_half)
    g_b = jnp.where(
        c == 0, jnp.concatenate([g_half, g_rest]), jnp.concatenate([g_rest, g_half])
    )
    base = [dot_t(k, g_a) for k in keep]
    mid = jnp.where(end, e2, m_own)

    def going(k):
        return (base[k][256:] + dot_t(x_b[k][:, 256:], g_b)).astype(bf16)

    def staying(k):
        return base[k][:256] + dot_t(x_b[k][:, :256], g_b)

    def cat(*arrays):
        return jnp.concatenate(arrays, axis=-1)

    x_b.append(beside(after(leave[1], x_b[0])))
    e3 = line(after(m2, e2, x_b[0]), ENDS_OUT)
    m3 = line(after(q_own, m2, x_b[0]), MIDDLE)
    q3 = across(after(going(0), q2))
    drift.take(drift.send(m3))
    rows = [None, None, jnp.concatenate([e_own, q2]), jnp.concatenate([w, q_own])]
    k_a = dot(cat(keep[2], keep[3]), jnp.concatenate(rows[2:]))
    part0 = staying(0) + q3.astype(f32)

    x_b.append(beside(after(leave[2], x_b[1])))
    e4 = line(after(jnp.where(end, part0.astype(bf16), m3), e3, x_b[1]), PAIRS)
    m4 = line(after(q2, m3, x_b[1]), MIDDLE)
    q4 = across(after(going(1), q3))
    drift.take(drift.send(m4))
    part1 = staying(1) + q4.astype(f32)

    x_b.append(beside(after(leave[3], x_b[2])))
    e5 = line(after(jnp.where(end, part1.astype(bf16), m4), e4, x_b[2]), PAIRS)
    m5 = line(after((part0 + e4.astype(f32)).astype(bf16), m4, x_b[2]), MIDDLE)
    q5 = across(after(going(2), q4))
    drift.take(drift.send(q4))
    rows[1] = jnp.concatenate([mid, jnp.where(end, e4, m3)])
    k_a = k_a + dot(keep[1], rows[1])
    k_b = dot(cat(x_b[1], x_b[2]), jnp.concatenate(rows[1:3]))
    part2 = staying(2) + q5.astype(f32)
    (x_b[3], e5, m5, q5), drift.v, part1, part2, k_a, k_b = together(
        (x_b[3], e5, m5, q5), drift.v, part1, part2, k_a, k_b
    )

    got = (
        line((part2 + m5.astype(f32)).astype(bf16), PAIRS),
        line((part1 + e5.astype(f32)).astype(bf16), MIDDLE),
        across(going(3)),
    )
    rows[0] = jnp.concatenate([jnp.where(end, e3, m2), jnp.where(end, e5, m4)])
    k_a = k_a + dot(keep[0], rows[0])
    k_b = k_b + dot(cat(x_b[0], x_b[3]), jnp.concatenate([rows[0], rows[3]]))
    k_got = core(jnp.where(stays, k_b, k_a).astype(bf16))
    keys_work = (jnp.where(stays, k_a, k_b) + k_got.astype(f32)).astype(bf16)
    keys = jnp.where(stays, keys_work, swap(keys_work))
    e6, m6, q6 = got
    total = staying(3) + q6.astype(f32) + e6.astype(f32) + m6.astype(f32)
    gradient = jnp.where(stays, total, swap(total.astype(bf16)).astype(f32))
    drift.take(drift.send())

    new_first = first_decay * adam_first[0] + (1.0 - first_decay) * gradient
    new_second = second_decay * adam_second[0] + (1.0 - second_decay) * gradient * gradient
    master = weight.astype(f32)
    update = new_first / (jnp.sqrt(new_second) + adam_floor) + weight_decay * master
    new_weight = (master - learn_rate * update).astype(bf16)

    mean = drift.v / 16
    new_momentum = outer_decay * outer_momentum + mean
    new_anchor = anchor - outer_rate * (mean + outer_decay * new_momentum)
    return (keys, new_weight[None], new_first[None], new_second[None], new_anchor, new_momentum)


def solution(mesh):
    fine = Mesh(mesh.devices.reshape(2, 4, 2, 4, 4), ("zh", "y", "c", "zl", "x"))
    replica, fsdp = ("zh", "y", "c"), ("zl", "x")
    tokens, stacked, shared = P(replica + fsdp, None), P(replica, fsdp, None), P(fsdp, None)
    return jax.shard_map(
        on_device,
        mesh=fine,
        in_specs=(tokens, tokens, stacked, stacked, stacked, stacked, shared, shared),
        out_specs=(tokens, stacked, stacked, stacked, shared, shared),
        check_vma=False,
    )
```

```python
import jax
import jax.numpy as jnp
from jax import lax
from jax.experimental import pallas as pl
from jax.experimental.pallas import tpu as pltpu
from jax.sharding import Mesh, PartitionSpec as P

learn_rate = 0.001
weight_decay = 0.1
first_decay = 0.9
second_decay = 0.95
adam_floor = 1e-08
outer_rate = 0.7
outer_decay = 0.9

bf16, f32 = jnp.bfloat16, jnp.float32

HOME = (0, 1, 1, 0)
SWAP = [(c * 4 + x, (1 - c) * 4 + (x ^ 1)) for c in range(2) for x in range(4) if c != HOME[x]]
CORE = [(0, 1), (1, 0)]
ACROSS = [(x, 3 - x) for x in range(4)]
BESIDE = [(x, x ^ 1) for x in range(4)]
ENDS_OUT = [(1, 0), (2, 3)]
PAIRS = [(0, 1), (1, 0), (2, 3), (3, 2)]
MIDDLE = [(1, 2), (2, 1)]
ORDER = ((3, 2, 1, 0), (3, 2, 0, 1), (0, 1, 3, 2), (0, 1, 2, 3))


def swap(v):
    return lax.ppermute(v, ("c", "x"), SWAP)


def core(v):
    return lax.ppermute(v, "c", CORE)


def beside(v):
    return lax.ppermute(v, "x", BESIDE)


def across(v):
    return lax.ppermute(v, "x", ACROSS)


def line(v, pairs):
    return lax.ppermute(v, "zl", pairs)


def dot(a, b):
    return jnp.dot(a, b, preferred_element_type=f32)


def dot_t(a, b):
    return lax.dot_general(a, b, (((0,), (0,)), ((), ())), preferred_element_type=f32)


def together(*arrays):
    return lax.optimization_barrier(arrays)


def after(array, *earlier):
    return together(array, *earlier)[0]


def move(_, a0, a1, b0, b1, to_a, to_b):
    to_a[0, :, :256] = a0[...]
    to_a[0, :, 256:] = a1[...]
    to_b[0, :, :256] = b0[...]
    to_b[0, :, 256:] = b1[...]


def halves(tokens, blocks):
    def spec(half, place):
        return pl.BlockSpec((512, 256), lambda n, table: (0, table[half, 2 * n + place]))

    out = pl.BlockSpec((1, 512, 512), lambda n, table: (n, 0, 0))
    kind = jax.ShapeDtypeStruct((4, 512, 512), bf16)
    return pl.pallas_call(
        move,
        grid_spec=pltpu.PrefetchScalarGridSpec(
            num_scalar_prefetch=1,
            grid=(4,),
            in_specs=[spec(half, place) for half in range(2) for place in range(2)],
            out_specs=[out, out],
        ),
        out_shape=[kind, kind],
        cost_estimate=pl.CostEstimate(flops=0, bytes_accessed=16 << 20, transcendentals=0),
    )(blocks, tokens, tokens, tokens, tokens)


class Drift:
    def __init__(self, own, c, y):
        near = [(i, i ^ 1) for i in range(4)]
        wide = [(i, i ^ 2) for i in range(4)]
        self.v = own
        self.steps = [("c", CORE, c), ("y", near, y % 2), ("y", wide, y // 2), ("zh", CORE, c)]
        self.at = 0

    def send(self, *earlier):
        self.v = after(self.v, *earlier)
        if self.at < 3:
            bit = self.steps[self.at][2]
            n = self.v.shape[0] // 2
            self.sent = lax.dynamic_slice_in_dim(self.v, (1 - bit) * n, n, 0)
        elif self.at == 3:
            (self.sent,) = together(self.v.astype(bf16))
        else:
            self.sent = self.v
        axis, perm, _ = self.steps[min(self.at, 6 - self.at)]
        return lax.ppermute(self.sent, axis, perm)

    def take(self, got):
        bit = self.steps[min(self.at, 6 - self.at)][2]
        v = self.v
        if self.at < 3:
            n = v.shape[0] // 2
            self.v = lax.dynamic_slice_in_dim(v, bit * n, n, 0) + got
        elif self.at == 3:
            self.v = self.sent.astype(f32) + got.astype(f32)
        else:
            self.v = jnp.where(bit == 0, jnp.concatenate([v, got]), jnp.concatenate([got, v]))
        self.at += 1


def on_device(
    tokens, key_grad, key_weight, adam_first, adam_second, local_params, anchor, outer_momentum
):
    c, x, z, y = (lax.axis_index(a) for a in ("c", "x", "zl", "y"))
    weight = key_weight[0]
    stays = c == jnp.where((x == 1) | (x == 2), 1, 0)
    end = (z == 0) | (z == 3)
    mine = jnp.where(x < 2, c, 3 - c)
    theirs = jnp.where(x < 2, 1 - c, 2 + c)
    order = [
        jnp.where(z < 2, 3, 0),
        jnp.where(z < 2, 2, 1),
        jnp.where(z == 0, 1, jnp.where(z == 1, 0, jnp.where(z == 2, 3, 2))),
        z,
    ]
    blocks = jnp.stack(
        [4 * order[k] + q for half in (theirs, mine) for k in range(4) for q in (half, 3 - half)]
    ).reshape(2, 8)

    drift = Drift(anchor - local_params[0].astype(f32), c, y)
    g_sib = core(key_grad)
    x_give, x_own = halves(tokens, after(blocks.astype(jnp.int32), g_sib))
    w, g_sib, d, x_give, x_own, drift.v = together(
        swap(weight), g_sib, drift.send(), x_give, x_own, drift.v
    )
    drift.take(d)
    w = jnp.where(stays, weight, w)
    g_a = jnp.where(stays, key_grad, g_sib)
    g_l = lax.dynamic_slice_in_dim(jnp.where(stays, g_sib, key_grad), c * 256, 256, 0)
    x_sib = core(x_give)

    got = (beside(g_l), line(w, PAIRS), line(w, MIDDLE), across(w), drift.send())
    leave = [jnp.where(stays, x_sib[k], x_own[k]) for k in range(4)]
    keep = [jnp.where(stays, x_own[k], x_sib[k]) for k in range(4)]
    got, leave, drift.v = together(got, leave, drift.v)
    g_half, e_own, m_own, q_own, d = got
    drift.take(d)

    x_b = [beside(leave[0])]
    e2, m2, q2 = line(m_own, ENDS_OUT), line(e_own, MIDDLE), across(e_own)
    drift.take(drift.send(m2))
    g_rest = core(g_half)
    g_b = jnp.where(
        c == 0, jnp.concatenate([g_half, g_rest]), jnp.concatenate([g_rest, g_half])
    )
    base = [dot_t(k, g_a) for k in keep]
    mid = jnp.where(end, e2, m_own)

    def going(k):
        return (base[k][256:] + dot_t(x_b[k][:, 256:], g_b)).astype(bf16)

    def staying(k):
        return base[k][:256] + dot_t(x_b[k][:, :256], g_b)

    def cat(*arrays):
        return jnp.concatenate(arrays, axis=-1)

    x_b.append(beside(after(leave[1], x_b[0])))
    e3 = line(after(m2, e2, x_b[0]), ENDS_OUT)
    m3 = line(after(q_own, m2, x_b[0]), MIDDLE)
    q3 = across(after(going(0), q2))
    drift.take(drift.send(m3))
    rows = [None, None, jnp.concatenate([e_own, q2]), jnp.concatenate([w, q_own])]
    k_a = dot(cat(keep[2], keep[3]), jnp.concatenate(rows[2:]))
    part0 = staying(0) + q3.astype(f32)

    x_b.append(beside(after(leave[2], x_b[1])))
    e4 = line(after(jnp.where(end, part0.astype(bf16), m3), e3, x_b[1]), PAIRS)
    m4 = line(after(q2, m3, x_b[1]), MIDDLE)
    q4 = across(after(going(1), q3))
    drift.take(drift.send(m4))
    part1 = staying(1) + q4.astype(f32)

    x_b.append(beside(after(leave[3], x_b[2])))
    e5 = line(after(jnp.where(end, part1.astype(bf16), m4), e4, x_b[2]), PAIRS)
    m5 = line(after((part0 + e4.astype(f32)).astype(bf16), m4, x_b[2]), MIDDLE)
    q5 = across(after(going(2), q4))
    drift.take(drift.send(q4))
    rows[1] = jnp.concatenate([mid, jnp.where(end, e4, m3)])
    k_a = k_a + dot(keep[1], rows[1])
    k_b = dot(cat(x_b[1], x_b[2]), jnp.concatenate(rows[1:3]))
    part2 = staying(2) + q5.astype(f32)
    (x_b[3], e5, m5, q5), drift.v, part1, part2, k_a, k_b = together(
        (x_b[3], e5, m5, q5), drift.v, part1, part2, k_a, k_b
    )

    got = (
        line((part2 + m5.astype(f32)).astype(bf16), PAIRS),
        line((part1 + e5.astype(f32)).astype(bf16), MIDDLE),
        across(going(3)),
    )
    rows[0] = jnp.concatenate([jnp.where(end, e3, m2), jnp.where(end, e5, m4)])
    k_a = k_a + dot(keep[0], rows[0])
    k_b = k_b + dot(cat(x_b[0], x_b[3]), jnp.concatenate([rows[0], rows[3]]))
    k_got = core(jnp.where(stays, k_b, k_a).astype(bf16))
    keys_work = (jnp.where(stays, k_a, k_b) + k_got.astype(f32)).astype(bf16)
    keys = jnp.where(stays, keys_work, swap(keys_work))
    e6, m6, q6 = got
    total = staying(3) + q6.astype(f32) + e6.astype(f32) + m6.astype(f32)
    gradient = jnp.where(stays, total, swap(total.astype(bf16)).astype(f32))
    drift.take(drift.send())

    new_first = first_decay * adam_first[0] + (1.0 - first_decay) * gradient
    new_second = second_decay * adam_second[0] + (1.0 - second_decay) * gradient * gradient
    master = weight.astype(f32)
    update = new_first / (jnp.sqrt(new_second) + adam_floor) + weight_decay * master
    new_weight = (master - learn_rate * update).astype(bf16)

    mean = drift.v / 16
    new_momentum = outer_decay * outer_momentum + mean
    new_anchor = anchor - outer_rate * (mean + outer_decay * new_momentum)
    return (keys, new_weight[None], new_first[None], new_second[None], new_anchor, new_momentum)


def solution(mesh):
    fine = Mesh(mesh.devices.reshape(2, 4, 2, 4, 4), ("zh", "y", "c", "zl", "x"))
    replica, fsdp = ("zh", "y", "c"), ("zl", "x")
    tokens, stacked, shared = P(replica + fsdp, None), P(replica, fsdp, None), P(fsdp, None)
    return jax.shard_map(
        on_device,
        mesh=fine,
        in_specs=(tokens, tokens, stacked, stacked, stacked, stacked, shared, shared),
        out_specs=(tokens, stacked, stacked, stacked, shared, shared),
        check_vma=False,
    )
```
